256 devices in a mesh: grp: 4 (over x), seq: 16 (over z, core), dp: 4 (over y).
Axes of the slice: x: 4, y: 4, z: 8, core: 2. Of those that a mesh axis runs over, the one named last changes fastest.
Arguments:
- item_hidden: bfloat16 [32768, 2048], P(('grp', 'seq', 'dp')), may hold values from -6 to 6
- item_gain: float32 [2048], replicated, may hold values from 0.25 to 1.75
- slot_owner: int32 [32, 1024, 1], P(('grp', 'dp'), 'seq'), may hold values from 0 to 63; in each aligned block of 64 rows (0 to 63, 64 to 127, ..., all dimensions but the last counted through in order) at most 2 rows name the same one
- slot_row: int32 [32, 1024], P(('grp', 'dp'), 'seq'), may hold values from 0 to 127
- seq_count: int32 [32], P(('grp', 'dp')), may hold values from 1 to 1024, 20480 in all
- user_gain: float32 [2048], replicated, may hold values from 0.25 to 1.75
- query_key_value_weight: bfloat16 [3, 2048, 2048], P(None, None, 'seq'), as said below
- d_out: bfloat16 [32, 1024, 2048], P(('grp', 'dp'), None, 'seq'), may hold values from -6 to 6
Outputs:
- attn_out: bfloat16 [32, 1024, 2048], P(('grp', 'dp'), None, 'seq')
- d_hidden: bfloat16 [32768, 2048], P(('grp', 'seq', 'dp'))
- grad_qkv: float32 [3, 2048, 2048], P(None, None, 'seq')
- grad_user_gain: float32 [2048], replicated
- grad_item_gain: float32 [2048], replicated
The draws below stay inside these ranges and needn't reach their ends.
Inputs may be any that keep to these rules, and one draw needn't show every extreme that they name: `slot_owner`: within each sequence, each aligned block of 64 positions names one owner at most 2 times; some block reaches it. `seq_count`: every sequence has one live slot or more, the live slots first. `query_key_value_weight`: projection weights of order fan-in to the minus one half.
All inputs are finite; a program needn't handle non-finite values. No bound on the sum of `seq_count` on one device may be relied on, other than what follows from the above.
Results may differ from the reference program's by a relative error of at most 0.025.
The reference program's roundings to bfloat16 on the way count: a program that leaves them out, or rounds other values in their place, can miss the bound.
Values may be sent and summed in bfloat16 or wider, within the bound.
A program may use at most 128 MiB of HBM per device.

```python
import math
import jax
import jax.numpy as jnp
import numpy as np
from jax import lax

HEADS = 16
HD = 128
EMBED_WIDTH = 2048
SLOT_COUNT = 1024
SPG = 2
ITEMS_DEV = 128
SEQS = 32
ITEMS = 32768
OWNERS = 64
BLOCK = 64
CAPH = 2
N_SEQ = 16
N_DP = 4


def draw_query_key_value_weight(key, part):
    key = jax.random.fold_in(key, 11)
    first = jax.random.fold_in(key, 0)
    base = jax.random.normal(first, (3, EMBED_WIDTH, EMBED_WIDTH), jnp.float32) * EMBED_WIDTH ** (-0.5)
    return base.astype(jnp.bfloat16)


def place_ends(values, own_key, low, high):
    longest = values.shape.index(max(values.shape))
    spots = []
    for shift in (0, 1):
        where = [jax.random.randint(jax.random.fold_in(own_key, axis), (), 0, length) for axis, length in enumerate(values.shape)]
        where[longest] = (where[longest] + shift) % values.shape[longest]
        spots.append(tuple(where))
    return values.at[spots[0]].set(low).at[spots[1]].set(high)


def level_of(own_key, dims, cuts, least, high):
    loudness = 1.0
    for dim, parts in cuts:
        heights = jax.random.uniform(jax.random.fold_in(jax.random.fold_in(own_key, 6), dim), (parts,), jnp.float32, least / len(cuts), high / len(cuts))
        loudness = loudness * jnp.repeat(jnp.exp(heights), dims[dim] // parts).reshape((-1,) + (1,) * (len(dims) - 1 - dim))
    return loudness


def split_up(amount, total, most, skew):
    weights = [(1 << 20) // math.isqrt(standing ** skew) + 1 for standing in range(2, amount + 1)]
    rest, holding = total - most - (amount - 1), [1] * (amount - 1)
    while rest > 0:
        candidates = [i for i in range(amount - 1) if holding[i] < most]
        whole, left = sum([weights[i] for i in candidates]), rest
        for i in candidates:
            addition = min(most - holding[i], max(1, left * weights[i] // whole), rest)
            holding[i] = holding[i] + addition
            rest = rest - addition
    return np.array([most] + holding)


def uneven_parts(rng, amount, total, reach, slope):
    if amount == 2:
        one = jax.random.randint(rng, (), max(1, total - reach), min(reach, total - 1) + 1)
        return jnp.stack([one, total - one])
    sizes = jnp.asarray(split_up(amount, total, reach, slope), jnp.int32)
    twos = (amount - 1) // 2
    donor, taker = sizes[1:1 + 2 * twos:2], sizes[2:2 + 2 * twos:2]
    room = jnp.minimum(donor - 1, reach - taker)
    moved = jax.random.randint(jax.random.fold_in(rng, 1), (twos,), 0, 1 << 20) % (room + 1)
    sizes = sizes.at[1:1 + 2 * twos:2].set(donor - moved).at[2:2 + 2 * twos:2].set(taker + moved)
    return sizes[jax.random.permutation(jax.random.fold_in(rng, 2), amount)]


def assign_block(stream_key, own, number, rows, number_of, top, bound, slope):
    sequence = jax.random.permutation(stream_key, number_of)
    crowded, common = load_shares(number_of, rows * top, bound, slope, True), load_shares(number_of, rows * top, bound, slope, False)
    places = jnp.arange(number_of)

    def named(sizes, rotation):
        used = int((sizes > 0).sum())
        fixed = max(1, used // 4)
        moved = fixed + (places - fixed + rotation * (used - fixed)) % max(1, number_of - fixed)
        return jnp.zeros((number_of,), jnp.int32).at[sequence[jnp.where(places < fixed, places, moved)]].set(jnp.asarray(sizes, jnp.int32))

    sizes = jnp.where(number % 4 == 0, named(crowded, number // 4), named(common, number - number // 4 - 1))
    mixed = jax.random.permutation(jax.random.fold_in(own, 3), number_of)
    source_of, receiver = mixed[0:number_of // 2 * 2:2], mixed[1:number_of // 2 * 2:2]
    room = jnp.minimum(sizes[source_of] - 1, bound - sizes[receiver]) // 2
    room = jnp.where((source_of == sequence[0]) | (receiver == sequence[0]) | (sizes[receiver] == 0), 0, jnp.maximum(room, 0))
    moved = jax.random.randint(jax.random.fold_in(own, 4), (number_of // 2,), 0, 1 << 20) % (room + 1)
    sizes = sizes.at[source_of].add(-moved).at[receiver].add(moved)
    members = jnp.searchsorted(jnp.cumsum(sizes), jnp.arange(rows * top), side="right").astype(jnp.int32)
    listing = members.reshape(top, rows).T
    listing = listing[jax.random.permutation(jax.random.fold_in(own, 1), rows)]
    rotation = jax.random.randint(jax.random.fold_in(own, 2), (rows, 1), 0, top)
    return jnp.take_along_axis(listing, (jnp.arange(top)[None, :] + rotation) % top, axis=1)


def load_shares(amount, total, most, slope, full):
    portions = [(1 << 20) // math.isqrt(grade ** slope) + 1 for grade in range(1, amount + 1)]
    largest = most if full else min(most, max(-(-total // amount), total * portions[0] // sum(portions)))
    least = 1 if total - largest >= amount - 1 else 0
    given, rest = [largest] + [least] * (amount - 1), total - largest - least * (amount - 1)
    while rest > 0:
        free = [i for i in range(1, amount) if given[i] < largest] or [i for i in range(1, amount) if given[i] < most]
        whole, remaining = sum([portions[i] for i in free]), rest
        for i in free:
            addition = min(most - given[i], max(1, remaining * portions[i] // whole), rest)
            given[i] = given[i] + addition
            rest = rest - addition
    return np.array(given)


def gaussian(key, extent, deviation, most, cuts=(), kind=jnp.bfloat16):
    values = deviation * jax.random.normal(key, extent, jnp.float32)
    if cuts:
        values = values * level_of(key, extent, cuts, -0.22, 0.18)
    return jnp.clip(values, -most, most).astype(kind)


def setup_inputs(seed: int = 0) -> dict:
    key_list = jax.random.split(jax.random.key(seed), 9)
    item_hidden = gaussian(key_list[0], (ITEMS, EMBED_WIDTH), 1.0, 6.0, ((0, 256),))
    item_gain = jnp.clip(1.0 + 0.15 * jax.random.normal(key_list[1], (EMBED_WIDTH,), jnp.float32), 0.25, 1.75)
    slot_owner_keys = jax.random.split(jax.random.fold_in(key_list[2], 1), SEQS * SLOT_COUNT // BLOCK)
    slot_owner_turns = jax.random.permutation(jax.random.fold_in(key_list[2], 3), SEQS * SLOT_COUNT // BLOCK)
    slot_owner = jax.vmap(lambda own, number: assign_block(jax.random.fold_in(key_list[2], 2), own, number, BLOCK, OWNERS, 1, CAPH, 2))(slot_owner_keys, slot_owner_turns).reshape((SEQS, SLOT_COUNT, 1))
    slot_row = place_ends(jax.random.randint(key_list[3], (SEQS, SLOT_COUNT), 0, ITEMS_DEV), jax.random.fold_in(key_list[3], 1), 0, ITEMS_DEV - 1).astype(jnp.int32)
    seq_count = uneven_parts(key_list[4], SEQS, SEQS * SLOT_COUNT * 5 // 8, SLOT_COUNT, 2).astype(jnp.int32)
    user_gain = jnp.clip(1.0 + 0.15 * jax.random.normal(key_list[5], (EMBED_WIDTH,), jnp.float32), 0.25, 1.75)
    query_key_value_weight = draw_query_key_value_weight(jax.random.fold_in(key_list[8], 71), 0)
    d_out = gaussian(key_list[7], (SEQS, SLOT_COUNT, EMBED_WIDTH), 1.0, 6.0, ((0, 16), (2, 16)))
    return {"item_hidden": item_hidden, "item_gain": item_gain, "slot_owner": slot_owner, "slot_row": slot_row, "seq_count": seq_count, "user_gain": user_gain, "query_key_value_weight": query_key_value_weight, "d_out": d_out}


epsilon = 1e-05

def norm_rows(values, gain_row):
    factor = lax.rsqrt(lax.optimization_barrier(jnp.mean(values * values, axis=-1, keepdims=True)) + epsilon)
    return (values * factor * gain_row, factor)

def norm_back(values, factor, gain_row, incoming):
    weighted = gain_row * incoming
    return factor * weighted - values * factor * factor * factor * lax.optimization_barrier(jnp.mean(weighted * values, axis=-1, keepdims=True))

def head_math(query, keys, values, upstream, live_count):
    length = query.shape[0]
    factor = 1.0 / math.sqrt(query.shape[-1])
    query_f = query.astype(jnp.float32)
    keys_f = keys.astype(jnp.float32)
    values_f = values.astype(jnp.float32)
    upstream_f = upstream.astype(jnp.float32)
    scores = jnp.einsum('qhd,khd->hqk', query_f, keys_f) * factor
    places = jnp.arange(length, dtype=jnp.int32)
    allowed = (places[None, :] <= places[:, None]) & (places[None, :] < live_count)
    scores = jnp.where(allowed[None], scores, -1e+30)
    highest = lax.optimization_barrier(jnp.max(scores, axis=-1, keepdims=True))
    exponent = jnp.exp(scores - highest)
    weights_f = exponent / lax.optimization_barrier(jnp.sum(exponent, axis=-1, keepdims=True))
    weights_b = weights_f.astype(jnp.bfloat16).astype(jnp.float32)
    result = jnp.einsum('hqk,khd->qhd', weights_b, values_f).astype(jnp.bfloat16)
    d_weights = jnp.einsum('qhd,khd->hqk', upstream_f, values_f)
    d_values = jnp.einsum('hqk,qhd->khd', weights_b, upstream_f).astype(jnp.bfloat16)
    center = lax.optimization_barrier(jnp.sum(weights_f * d_weights, axis=-1, keepdims=True))
    d_scores = (weights_f * (d_weights - center) * factor).astype(jnp.bfloat16).astype(jnp.float32)
    d_query = jnp.einsum('hqk,khd->qhd', d_scores, keys_f).astype(jnp.bfloat16)
    d_keys = jnp.einsum('hqk,qhd->khd', d_scores, query_f).astype(jnp.bfloat16)
    return (result, d_query, d_keys, d_values)

def reference(item_hidden, item_gain, slot_owner, slot_row, seq_count, user_gain, query_key_value_weight, d_out):
    hidden_f = item_hidden.astype(jnp.float32)
    item_normed, item_factor = norm_rows(hidden_f, item_gain)
    embedded = item_normed.astype(jnp.bfloat16)
    owners = N_SEQ * N_DP
    group_of = jnp.arange(SEQS, dtype=jnp.int32) // (SPG * N_DP)
    item_index = (group_of[:, None] * owners + slot_owner[:, :, 0]) * ITEMS_DEV + slot_row
    inputs = embedded[item_index]
    inputs_f = inputs.astype(jnp.float32)
    user_normed, user_factor = norm_rows(inputs_f, user_gain)
    normed = user_normed.astype(jnp.bfloat16)
    w_float = query_key_value_weight.astype(jnp.float32)
    split_weight = w_float.reshape(3, EMBED_WIDTH, N_SEQ, EMBED_WIDTH // N_SEQ)

    def per_seq(running, packed):
        normed_seq, live_count, upstream = packed
        projected = jnp.einsum('ld,cde->lce', normed_seq.astype(jnp.float32), w_float).astype(jnp.bfloat16)
        projected = projected.reshape(SLOT_COUNT, 3, HEADS, HD)
        result, d_query, d_keys, d_values = head_math(projected[:, 0], projected[:, 1], projected[:, 2], upstream.reshape(SLOT_COUNT, HEADS, HD), live_count)
        projection_gradient = jnp.stack([d_query, d_keys, d_values], axis=1).astype(jnp.float32)
        partial_totals_sum = jnp.einsum('ijmz,jnmz->min', projection_gradient.reshape(SLOT_COUNT, 3, N_SEQ, EMBED_WIDTH // N_SEQ), split_weight)
        rounded = lax.optimization_barrier(partial_totals_sum.astype(jnp.bfloat16))
        d_normed = lax.optimization_barrier(jnp.sum(rounded.astype(jnp.float32), axis=0))
        grad_w = running + jnp.einsum('ld,lce->cde', normed_seq.astype(jnp.float32), projection_gradient.reshape(SLOT_COUNT, 3, EMBED_WIDTH))
        return (grad_w, (result.reshape(SLOT_COUNT, EMBED_WIDTH), d_normed))
    grad_qkv, (attn_out, d_normed) = lax.scan(per_seq, jnp.zeros((3, EMBED_WIDTH, EMBED_WIDTH), jnp.float32), (normed, seq_count, d_out))
    grad_user_gain = lax.optimization_barrier(jnp.sum(d_normed * inputs_f * user_factor, axis=(0, 1)))
    d_inputs = norm_back(inputs_f, user_factor, user_gain, d_normed)
    d_embedded = jax.ops.segment_sum(d_inputs.reshape(-1, EMBED_WIDTH), item_index.reshape(-1), num_segments=ITEMS)
    grad_item_gain = lax.optimization_barrier(jnp.sum(d_embedded * hidden_f * item_factor, axis=0))
    d_hidden = norm_back(hidden_f, item_factor, item_gain, d_embedded).astype(jnp.bfloat16)
    return (attn_out, d_hidden, grad_qkv, grad_user_gain, grad_item_gain)
```

```python
import functools
import math

import jax
import jax.numpy as jnp
from jax import lax
from jax.experimental import pallas as pl
from jax.experimental.pallas import tpu as pltpu
from jax.sharding import PartitionSpec as P

HD = 128
LANES = 128
Q = 4
EPS = 1e-05
MESH = pl.DeviceIdType.MESH
F32, BF16 = jnp.float32, jnp.bfloat16
VMEM_LIMIT = 60 * 2**20


def iota(shape, dim):
    return lax.broadcasted_iota(jnp.int32, shape, dim).astype(F32)


def onehot(mask):
    return jnp.where(mask, 1.0, 0.0).astype(BF16)


def column(row):
    return jnp.broadcast_to(row, (LANES, LANES)).T


def plane_peer(index, nd):
    return {"seq": index // nd, "dp": lax.rem(index, nd)}


def greet(barrier, device):
    pl.semaphore_signal(barrier, inc=1, device_id=device, device_id_type=MESH)


def remote(src, dst, send, recv, device):
    return pltpu.make_async_remote_copy(
        src_ref=src, dst_ref=dst, send_sem=send, recv_sem=recv, device_id=device, device_id_type=MESH
    )


def slots(ids_ref, cap):
    owner_row = ids_ref[0:1, :].astype(F32)
    owner = jnp.broadcast_to(owner_row, (LANES, LANES))
    same = jnp.where(owner == owner.T, 1.0, 0.0)
    before = iota((LANES, LANES), 0) < iota((LANES, LANES), 1)
    rank_row = jnp.sum(jnp.where(before, same, 0.0), axis=0, keepdims=True)
    return owner_row, rank_row, (owner_row * cap + rank_row) * Q


def fetch_kernel(
    ns, nd, cap, ids_ref, hidden_ref, igain_ref, ugain_ref,
    normed_ref, inputs_ref, ufactor_ref, val_ref,
    req, reqr, table, out, arr, id_send, id_recv, row_send, row_recv,
):
    owners, msg = ns * nd, cap * Q
    per = LANES // msg
    groups = owners // per
    width = hidden_ref.shape[1]
    part = width // Q
    items = hidden_ref.shape[0]
    me = lax.axis_index("seq") * nd + lax.axis_index("dp")
    barrier = pltpu.get_barrier_semaphore()

    @pl.loop(1, owners)
    def _(i):
        greet(barrier, plane_peer(lax.rem(me + i, owners), nd))

    owner_row, rank_row, base_row = slots(ids_ref, cap)
    lane = lax.broadcasted_iota(jnp.int32, (LANES, LANES), 1)
    slot_in = ((lane % msg) // Q).astype(F32)
    piece = (lane % Q).astype(F32)
    row_col = column(ids_ref[1:2, :].astype(F32) + 1.0)
    rank_col = column(rank_row)
    wanted = jnp.where(rank_col == slot_in, row_col, 0.0).astype(BF16)
    names = onehot(iota((owners, LANES), 0) == owner_row)
    asked = jnp.dot(names, wanted, preferred_element_type=F32)
    asked = jnp.where(asked > 0.5, asked - 1.0 + piece[0:1, :] * items, -1.0).astype(jnp.int32)
    for o in range(owners):
        req[o] = asked[o : o + 1, :]

    pl.semaphore_wait(barrier, owners - 1)

    @pl.loop(1, owners)
    def _(i):
        peer = lax.rem(me + i, owners)
        remote(req.at[peer], reqr.at[me], id_send, id_recv, plane_peer(peer, nd)).start()

    reqr[me] = req[me]
    hidden = hidden_ref[...].astype(F32)
    factor = lax.rsqrt(jnp.mean(hidden * hidden, axis=-1, keepdims=True) + EPS)
    for q in range(Q):
        cols = slice(q * part, (q + 1) * part)
        piece_f = hidden_ref[:, cols].astype(F32)
        table[q * items : (q + 1) * items, :] = (piece_f * factor * igain_ref[:, cols]).astype(BF16)
    remote(
        req.at[pl.ds(0, owners - 1)], reqr.at[pl.ds(0, owners - 1)], id_send, id_recv, plane_peer(me, nd)
    ).wait()

    lane_group = lax.broadcasted_iota(jnp.int32, (1, LANES), 1) // msg
    my_group = me // per
    for step in range(groups):
        turn = (step + 1) // 2 if step % 2 else groups - step // 2
        g = lax.rem(my_group + turn, groups)
        val = jnp.zeros((1, LANES), jnp.int32)
        for k in range(per):
            val = jnp.where(lane_group == k, reqr[g * per + k], val)
        val_ref[g] = val
        col = column(val.astype(F32))
        pick = jnp.concatenate([onehot(col == iota((LANES, LANES), 1) + q * items) for q in range(Q)], axis=1)
        picked = jnp.dot(pick, table[...], preferred_element_type=F32).astype(BF16)
        out[pl.ds(g * per, per)] = picked.reshape(per, msg, part)
        for k in range(per):
            peer = g * per + k

            @pl.when(peer != me)
            def _():
                remote(out.at[peer], arr.at[me], row_send, row_recv, plane_peer(peer, nd)).start()

    arr[me] = out[me]
    base_col = column(base_row)
    remote(
        out.at[pl.ds(0, owners - 1)], arr.at[pl.ds(0, owners - 1)], row_send, row_recv, plane_peer(me, nd)
    ).wait()
    arrived = arr[...].reshape(owners * msg, part)
    total = jnp.zeros((LANES, 1), F32)
    for q in range(Q):
        place = jnp.concatenate(
            [onehot(iota((LANES, LANES), 1) + t * LANES == base_col + q) for t in range(groups)], axis=1
        )
        rows = jnp.dot(place, arrived, preferred_element_type=F32)
        inputs_ref[:, q * part : (q + 1) * part] = rows.astype(BF16)
        total += jnp.sum(rows * rows, axis=-1, keepdims=True)
    ufactor = lax.rsqrt(total / width + EPS)
    ufactor_ref[...] = ufactor
    normed_ref[...] = (inputs_ref[...].astype(F32) * ufactor * ugain_ref[...]).astype(BF16)


def fetch(ns, nd, cap, ids, hidden, igain, ugain):
    items, width = hidden.shape
    owners, msg = ns * nd, cap * Q
    vmem = pl.BlockSpec(memory_space=pltpu.VMEM)
    return pl.pallas_call(
        functools.partial(fetch_kernel, ns, nd, cap),
        out_shape=(
            jax.ShapeDtypeStruct((LANES, width), BF16),
            jax.ShapeDtypeStruct((LANES, width), BF16),
            jax.ShapeDtypeStruct((LANES, 1), F32),
            jax.ShapeDtypeStruct((owners * msg // LANES, 1, LANES), jnp.int32),
        ),
        in_specs=[vmem] * 4,
        out_specs=[vmem] * 4,
        scratch_shapes=[
            pltpu.VMEM((owners, 1, LANES), jnp.int32),
            pltpu.VMEM((owners, 1, LANES), jnp.int32),
            pltpu.VMEM((Q * items, width // Q), BF16),
            pltpu.VMEM((owners, msg, width // Q), BF16),
            pltpu.VMEM((owners, msg, width // Q), BF16),
        ]
        + [pltpu.SemaphoreType.DMA] * 4,
        compiler_params=pltpu.CompilerParams(
            collective_id=0, has_side_effects=True, vmem_limit_bytes=VMEM_LIMIT
        ),
        name="fetch",
    )(ids, hidden, igain, ugain)


def layer_kernel(
    ns, count_ref, normed_ref, inputs_ref, ufactor_ref, ugain_ref, weight_ref, dout_ref,
    attn_ref, grad_ref, dinputs_ref, uterms_ref,
    gat, prj, dpr, dpt, wgt, part, mix, ring, dk_acc, dv_acc,
    ag_send, ag_recv, sb_send, sb_recv, mx_send, mx_recv, rs_send, rs_recv,
):
    seqs, _, local_len, width = gat.shape
    length = ns * local_len
    nz = ns // 2
    half = nz // 2
    hops = 2 * half - 1
    hl = local_len // 2
    per = 4
    tile = per * local_len
    tiles = ns // per
    me = lax.axis_index("seq")
    z, core = me // 2, lax.rem(me, 2)
    sib = {"seq": me + 1 - 2 * core}
    sib_index = me + 1 - 2 * core
    ahead = ({"seq": lax.rem(me + 2, ns)}, {"seq": lax.rem(me + ns - 2, ns)})
    scale = 1.0 / math.sqrt(HD)

    barrier = pltpu.get_barrier_semaphore()
    for device in (*ahead, sib):
        greet(barrier, device)
    for f in range(seqs):
        gat[f, me] = normed_ref[f * local_len : (f + 1) * local_len, :]
    pl.semaphore_wait(barrier, 3)

    def ag_place(f, d, e, origin):
        far = e // 2
        h = d if e == hops - 1 else e % 2
        block = lax.rem(origin + (ns - 2 * far if d == 0 else 2 * far), ns)
        return gat.at[f, block, pl.ds(h * hl, hl)]

    def ag_copy(f, d, e):
        ref = ag_place(f, d, e, me)
        return remote(ref, ref, ag_send.at[f, d, e], ag_recv.at[f, d, e], ahead[d])

    def ag_arrival(f, d, e, at):
        behind = lax.rem(at + (ns - 2 if d == 0 else 2), ns)
        return ag_place(f, d, e, behind)

    def ag_wait(f, d, e):
        ref = ag_arrival(f, d, e, me)
        remote(ref, ref, ag_send.at[f, d, e], ag_recv.at[f, d, e], ahead[d]).wait_recv()

    def sb_copy(f, n):
        ref = gat.at[f, me] if n == 0 else ag_arrival(f, (n - 1) % 2, (n - 1) // 2, me)
        return remote(ref, ref, sb_send.at[f, n], sb_recv.at[f, n], sib)

    def sb_wait(f, n):
        ref = gat.at[f, sib_index] if n == 0 else ag_arrival(f, (n - 1) % 2, (n - 1) // 2, sib_index)
        remote(ref, ref, sb_send.at[f, n], sb_recv.at[f, n], sib).wait_recv()

    def ag_begin(f):
        for e in range(min(2, hops)):
            for d in range(2):
                ag_copy(f, d, e).start()
        sb_copy(f, 0).start()

    def ag_event(f, d, e):
        ag_wait(f, d, e)
        if e + 2 < hops - 1:
            ag_copy(f, d, e + 2).start()
        elif e + 2 == hops - 1 + d:
            ag_copy(f, d, hops - 1).start()
        sb_copy(f, 1 + 2 * e + d).start()

    def ag_events(f):
        return [functools.partial(ag_event, f, d, e) for e in range(hops) for d in range(2)]

    def ag_end(f):
        for n in range(1 + 2 * hops):
            sb_wait(f, n)

    order = [(half, None)] + [(t, h) for t in range(half - 1, 0, -1) for h in range(2)]

    def rs_what(d, i):
        t, h = order[i]
        return t, d if h is None else h

    def chip(d, t):
        return lax.rem(z + (t if d == 0 else nz - t), nz)

    def rs_copy(f, d, i):
        t, h = rs_what(d, i)
        return remote(
            mix.at[f, chip(d, t), pl.ds(h * hl, hl)], ring.at[f, d, i], rs_send.at[f, d, i], rs_recv.at[f, d, i], ahead[d]
        )

    def mx_copy(f, k):
        return remote(part.at[f, 2 * k + 1 - core], mix.at[f, k], mx_send.at[f, k], mx_recv.at[f, k], sib)

    def own_sum(f, k):
        mix[f, k] = (mix[f, k].astype(F32) + part[f, 2 * k + core].astype(F32)).astype(BF16)

    def rs_begin(f):
        for k in range(nz):
            mx_copy(f, k).wait_recv()

    def rs_own(f, t):
        own_sum(f, chip(0, t))
        if 0 < t < half:
            own_sum(f, chip(1, t))
        if t == half:
            for d in range(2):
                rs_copy(f, d, 0).start()
        elif t > 0:
            for d in range(2):
                for i in range(len(order)):
                    if rs_what(d, i)[0] == t and rs_source(d, i) is None:
                        rs_copy(f, d, i).start()

    def rs_source(d, i):
        t, h = rs_what(d, i)
        for j in range(len(order)):
            if rs_what(d, j) == (t + 1, h):
                return j
        return None

    def rs_event(f, d, j):
        rs_copy(f, d, j).wait_recv()
        t, h = rs_what(d, j)
        if t == 1:
            return
        for i in range(len(order)):
            if rs_what(d, i) == (t - 1, h):
                rows = pl.ds(h * hl, hl)
                k = chip(d, t - 1)
                mix[f, k, rows] = (mix[f, k, rows].astype(F32) + ring[f, d, j].astype(F32)).astype(BF16)
                rs_copy(f, d, i).start()

    def rs_events(f):
        out = [functools.partial(rs_begin, f)]
        out += [functools.partial(rs_own, f, t) for t in range(half, -1, -1)]
        return out + [functools.partial(rs_event, f, d, j) for j in range(len(order)) for d in range(2)]

    def rs_end(f):
        total = mix[f, z].astype(F32)
        for h in range(2):
            rows = slice(h * hl, (h + 1) * hl)
            got = total[rows]
            for d in range(2):
                for i in range(len(order)):
                    if rs_what(d, i) == (1, h):
                        got = got + ring[f, d, i].astype(F32)
            at = slice(f * local_len + h * hl, f * local_len + (h + 1) * hl)
            values = inputs_ref[at, :].astype(F32)
            factor = ufactor_ref[at, :]
            term = jnp.sum(got * values * factor, axis=0, keepdims=True)
            if f == 0 and h == 0:
                uterms_ref[...] = term
            else:
                uterms_ref[...] += term
            weighted = ugain_ref[...] * got
            center = jnp.mean(weighted * values, axis=-1, keepdims=True)
            dinputs_ref[at, :] = (factor * weighted - values * (factor * factor * factor * center)).astype(BF16)

    def project(f, i):
        rows = gat[f, i * per : (i + 1) * per].reshape(tile, width)
        prj[f, i * tile : (i + 1) * tile, :] = jnp.dot(rows, wgt[...], preferred_element_type=F32).astype(BF16)

    def attend(f, i):
        keys_n = (i + 1) * tile
        at = slice(i * tile, (i + 1) * tile)
        query = prj[f, at, 0:HD]
        keys = prj[f, 0:keys_n, HD : 2 * HD]
        values = prj[f, 0:keys_n, 2 * HD : 3 * HD]
        upstream = dout_ref[f, at, :]
        over = (((1,), (1,)), ((), ()))
        down = (((0,), (0,)), ((), ()))
        scores = lax.dot_general(query, keys, over, preferred_element_type=F32) * scale
        p = lax.broadcasted_iota(jnp.int32, (tile, keys_n), 0) + i * tile
        k = lax.broadcasted_iota(jnp.int32, (tile, keys_n), 1)
        allowed = (k <= p) & (k < count_ref[f])
        scores = jnp.where(allowed, scores, -1e30)
        exponent = jnp.exp(scores - jnp.max(scores, axis=-1, keepdims=True))
        weights = exponent * (1.0 / jnp.sum(exponent, axis=-1, keepdims=True))
        weights_b = weights.astype(BF16)
        attn_ref[f, at, :] = jnp.dot(weights_b, values, preferred_element_type=F32).astype(BF16)
        d_weights = lax.dot_general(upstream, values, over, preferred_element_type=F32)
        center = jnp.sum(weights * d_weights, axis=-1, keepdims=True)
        d_scores = (weights * (d_weights - center) * scale).astype(BF16)
        dpr[f, at, 0:HD] = jnp.dot(d_scores, keys, preferred_element_type=F32).astype(BF16)
        d_values = lax.dot_general(weights_b, upstream, down, preferred_element_type=F32)
        d_keys = lax.dot_general(d_scores, query, down, preferred_element_type=F32)
        old = i * tile
        if i:
            dv_acc[0:old, :] += d_values[0:old]
            dk_acc[0:old, :] += d_keys[0:old]
        dv_acc[at, :] = d_values[old:]
        dk_acc[at, :] = d_keys[old:]

    def attended(f):
        dpr[f, :, HD : 2 * HD] = dk_acc[...].astype(BF16)
        dpr[f, :, 2 * HD : 3 * HD] = dv_acc[...].astype(BF16)

    def back(f, i):
        rows = dpr[f, i * tile : (i + 1) * tile, :]
        term = lax.dot_general(rows, wgt[...], (((1,), (1,)), ((), ())), preferred_element_type=F32)
        part[f, i * per : (i + 1) * per] = term.astype(BF16).reshape(per, local_len, width)
        for k in range(per // 2):
            mx_copy(f, i * per // 2 + k).start()

    def turned(f):
        dpt[:, f * length : (f + 1) * length] = dpr[f].T

    def grad(j):
        cols = slice(j * 2 * LANES, (j + 1) * 2 * LANES)
        got = jnp.zeros((dpt.shape[0], 2 * LANES), F32)
        for f in range(seqs):
            rows = gat[f, :, :, cols].reshape(length, 2 * LANES)
            got += jnp.dot(dpt[:, f * length : (f + 1) * length], rows, preferred_element_type=F32)
        for k in range(2):
            grad_ref[2 * j + k] = got[:, k * LANES : (k + 1) * LANES].astype(BF16)

    def sequence_work(f):
        work = [functools.partial(project, f, i) for i in range(tiles)]
        work += [functools.partial(attend, f, i) for i in range(tiles)]
        work += [functools.partial(attended, f)]
        return work + [functools.partial(back, f, i) for i in range(tiles)]

    def interleave(events, work):
        done = 0
        for n, event in enumerate(events):
            event()
            upto = (n + 1) * len(work) // len(events)
            for item in work[done:upto]:
                item()
            done = upto

    ag_begin(0)
    for c in range(3):
        wgt[:, c * HD : (c + 1) * HD] = weight_ref[c]
    events = ag_events(0)
    for event in events[:-4]:
        event()
    ag_begin(1)
    for event in events[-4:]:
        event()
    ag_end(0)
    interleave(ag_events(1), sequence_work(0))
    ag_end(1)
    interleave(rs_events(0), [functools.partial(turned, 0)] + sequence_work(1))
    rs_end(0)
    interleave(rs_events(1), [functools.partial(turned, 1)] + [functools.partial(grad, j) for j in range(width // (2 * LANES))])
    rs_end(1)
    for f in range(seqs):
        for d in range(2):
            for e in range(hops):
                ag_copy(f, d, e).wait_send()
                rs_copy(f, d, e).wait_send()
        for n in range(1 + 2 * hops):
            sb_copy(f, n).wait_send()
        for k in range(nz):
            mx_copy(f, k).wait_send()


def layer(ns, seqs, count, normed, inputs, ufactor, ugain, weight, dout):
    rows, width = normed.shape
    local_len = rows // seqs
    length = ns * local_len
    nz = ns // 2
    hops = nz - 1
    vmem = pl.BlockSpec(memory_space=pltpu.VMEM)
    cols = 3 * HD
    return pl.pallas_call(
        functools.partial(layer_kernel, ns),
        out_shape=(
            jax.ShapeDtypeStruct((seqs, length, HD), BF16),
            jax.ShapeDtypeStruct((width // LANES, cols, LANES), BF16),
            jax.ShapeDtypeStruct((rows, width), BF16),
            jax.ShapeDtypeStruct((1, width), F32),
        ),
        in_specs=[pl.BlockSpec(memory_space=pltpu.SMEM)] + [vmem] * 6,
        out_specs=[vmem] * 4,
        scratch_shapes=[
            pltpu.VMEM((seqs, ns, local_len, width), BF16),
            pltpu.VMEM((seqs, length, cols), BF16),
            pltpu.VMEM((seqs, length, cols), BF16),
            pltpu.VMEM((cols, seqs * length), BF16),
            pltpu.VMEM((width, cols), BF16),
            pltpu.VMEM((seqs, ns, local_len, width), BF16),
            pltpu.VMEM((seqs, nz, local_len, width), BF16),
            pltpu.VMEM((seqs, 2, hops, local_len // 2, width), BF16),
            pltpu.VMEM((length, HD), F32),
            pltpu.VMEM((length, HD), F32),
        ]
        + [pltpu.SemaphoreType.DMA((seqs, 2, hops))] * 2
        + [pltpu.SemaphoreType.DMA((seqs, 1 + 2 * hops))] * 2
        + [pltpu.SemaphoreType.DMA((seqs, nz))] * 2
        + [pltpu.SemaphoreType.DMA((seqs, 2, hops))] * 2,
        compiler_params=pltpu.CompilerParams(
            collective_id=1, has_side_effects=True, vmem_limit_bytes=VMEM_LIMIT
        ),
        name="layer",
    )(count, normed, inputs, ufactor, ugain, weight, dout)


def home_kernel(
    ng, ns, nd, cap, ids_ref, val_ref, hidden_ref, igain_ref, dinputs_ref, uterms_ref, grad_ref,
    dhidden_ref, gains_ref, full_ref,
    stack, out, arr, gin, tin, tin2, tsum,
    row_send, row_recv, gr_send, gr_recv, gg_send, gg_recv, t_send, t_recv, u_send, u_recv,
):
    owners, msg = ns * nd, cap * Q
    per = LANES // msg
    groups = owners // per
    items, width = hidden_ref.shape
    part = width // Q
    nr = ng * nd
    seq, dp, grp = lax.axis_index("seq"), lax.axis_index("dp"), lax.axis_index("grp")
    me = seq * nd + dp
    rep = grp * nd + dp
    barrier = pltpu.get_barrier_semaphore()

    def rep_peer(index):
        return {"grp": index // nd, "dp": lax.rem(index, nd)}

    @pl.loop(1, owners)
    def _(i):
        greet(barrier, plane_peer(lax.rem(me + i, owners), nd))

    @pl.loop(nd, nr)
    def _(i):
        greet(barrier, rep_peer(lax.rem(grp * nd + i, nr)))

    owner_row, rank_row, base_row = slots(ids_ref, cap)
    for q in range(Q):
        stack[q * LANES : (q + 1) * LANES, :] = dinputs_ref[:, q * part : (q + 1) * part]
    pl.semaphore_wait(barrier, owners - 1 + nr - nd)

    my_group = me // per
    gchunk = width // LANES // nr

    def grads_out(i):
        peer = lax.rem(rep + i, nr)
        remote(grad_ref.at[pl.ds(peer * gchunk, gchunk)], gin.at[rep], gr_send, gr_recv, rep_peer(peer)).start()

    for step in range(groups):
        turn = (step + 1) // 2 if step % 2 else groups - step // 2
        g = lax.rem(my_group + turn, groups)
        rows = iota((LANES, LANES), 0) + (g * LANES).astype(F32)
        place = jnp.concatenate([onehot(rows == base_row + q) for q in range(Q)], axis=1)
        sent = jnp.dot(place, stack[...], preferred_element_type=F32).astype(BF16)
        out[pl.ds(g * per, per)] = sent.reshape(per, msg, part)
        for k in range(per):
            peer = g * per + k

            @pl.when(peer != me)
            def _():
                remote(out.at[peer], arr.at[me], row_send, row_recv, plane_peer(peer, nd)).start()

        for i in range(1 + step * (nr - 1) // groups, 1 + (step + 1) * (nr - 1) // groups):
            grads_out(i)

    arr[me] = out[me]
    gin[rep] = grad_ref[pl.ds(rep * gchunk, gchunk)]
    remote(
        grad_ref.at[pl.ds(0, (nr - 1) * gchunk)], grad_ref.at[pl.ds(0, (nr - 1) * gchunk)], gr_send, gr_recv, rep_peer(rep)
    ).wait()
    got = gin[0].astype(F32)
    for i in range(1, nr):
        got += gin[i].astype(F32)
    mine = pl.ds(rep * gchunk, gchunk)
    full_ref[mine] = got.astype(BF16)

    @pl.loop(1, nr)
    def _(i):
        remote(full_ref.at[mine], full_ref.at[mine], gg_send, gg_recv, rep_peer(lax.rem(rep + i, nr))).start()

    hidden = hidden_ref[...].astype(F32)
    factor = lax.rsqrt(jnp.mean(hidden * hidden, axis=-1, keepdims=True) + EPS)
    remote(
        out.at[pl.ds(0, owners - 1)], arr.at[pl.ds(0, owners - 1)], row_send, row_recv, plane_peer(me, nd)
    ).wait()
    took = jnp.zeros((Q * items, part), F32)
    for g in range(groups):
        pick = onehot(iota((Q * items, LANES), 0) == val_ref[g].astype(F32))
        rows = arr[g * per : (g + 1) * per].reshape(LANES, part)
        took += jnp.dot(pick, rows, preferred_element_type=F32)
    center = jnp.zeros((items, 1), F32)
    terms = []
    for q in range(Q):
        cols = slice(q * part, (q + 1) * part)
        h = hidden_ref[:, cols].astype(F32)
        d = took[q * items : (q + 1) * items]
        center += jnp.sum(igain_ref[:, cols] * d * h, axis=-1, keepdims=True)
        tsum[q : q + 1, :] = jnp.sum(d * h * factor, axis=0, keepdims=True)
        tsum[Q + q : Q + q + 1, :] = uterms_ref[:, cols]
    center = center / width
    tin[seq] = tsum[...]

    @pl.loop(1, ns)
    def _(i):
        remote(tsum, tin.at[seq], t_send, t_recv, {"seq": lax.rem(seq + i, ns)}).start()

    for q in range(Q):
        cols = slice(q * part, (q + 1) * part)
        h = hidden_ref[:, cols].astype(F32)
        d = took[q * items : (q + 1) * items]
        dhidden_ref[:, cols] = (factor * igain_ref[:, cols] * d - h * (factor * factor * factor * center)).astype(BF16)

    remote(tin.at[pl.ds(0, ns - 1)], tin.at[pl.ds(0, ns - 1)], t_send, t_recv, {"seq": seq}).wait()
    total = tin[0]
    for i in range(1, ns):
        total = total + tin[i]
    tin2[rep] = total

    @pl.loop(1, nr)
    def _(i):
        remote(tin2.at[rep], tin2.at[rep], u_send, u_recv, rep_peer(lax.rem(rep + i, nr))).start()

    remote(tin2.at[pl.ds(0, nr - 1)], tin2.at[pl.ds(0, nr - 1)], u_send, u_recv, rep_peer(rep)).wait()
    total = tin2[0]
    for i in range(1, nr):
        total = total + tin2[i]
    gains_ref[...] = total
    remote(
        full_ref.at[pl.ds(0, (nr - 1) * gchunk)], full_ref.at[pl.ds(0, (nr - 1) * gchunk)], gg_send, gg_recv, rep_peer(rep)
    ).wait()


def home(ng, ns, nd, cap, ids, val, hidden, igain, dinputs, uterms, grads):
    items, width = hidden.shape
    owners, msg = ns * nd, cap * Q
    nr = ng * nd
    part = width // Q
    gchunk = width // LANES // nr
    vmem = pl.BlockSpec(memory_space=pltpu.VMEM)
    return pl.pallas_call(
        functools.partial(home_kernel, ng, ns, nd, cap),
        out_shape=(
            jax.ShapeDtypeStruct((items, width), BF16),
            jax.ShapeDtypeStruct((2 * Q, part), F32),
            jax.ShapeDtypeStruct(grads.shape, BF16),
        ),
        in_specs=[vmem] * 7,
        out_specs=[vmem] * 3,
        scratch_shapes=[
            pltpu.VMEM((Q * LANES, part), BF16),
            pltpu.VMEM((owners, msg, part), BF16),
            pltpu.VMEM((owners, msg, part), BF16),
            pltpu.VMEM((nr, gchunk, grads.shape[1], LANES), BF16),
            pltpu.VMEM((ns, 2 * Q, part), F32),
            pltpu.VMEM((nr, 2 * Q, part), F32),
            pltpu.VMEM((2 * Q, part), F32),
        ]
        + [pltpu.SemaphoreType.DMA] * 10,
        compiler_params=pltpu.CompilerParams(
            collective_id=2, has_side_effects=True, vmem_limit_bytes=VMEM_LIMIT
        ),
        name="home",
    )(ids, val, hidden, igain, dinputs, uterms, grads)


def local(
    item_hidden, item_gain, slot_owner, slot_row, seq_count, user_gain, query_key_value_weight, d_out
):
    ng, ns, nd = (lax.axis_size(a) for a in ("grp", "seq", "dp"))
    seqs, local_len, _ = slot_owner.shape
    width = item_hidden.shape[1]
    cap = seqs * max(2, 2 * local_len // (ns * nd))
    ids = jnp.stack([slot_owner.reshape(-1), slot_row.reshape(-1)])
    igain, ugain = item_gain.reshape(1, width), user_gain.reshape(1, width)
    normed, inputs, ufactor, val = fetch(ns, nd, cap, ids, item_hidden, igain, ugain)
    attn, grads, dinputs, uterms = layer(
        ns, seqs, seq_count, normed, inputs, ufactor, ugain, query_key_value_weight, d_out
    )
    d_hidden, gains, full = home(ng, ns, nd, cap, ids, val, item_hidden, igain, dinputs, uterms, grads)
    full = full.reshape(width // LANES, 3, HD, LANES).transpose(1, 0, 3, 2).reshape(3, width, HD)
    return (attn, d_hidden, full.astype(F32), gains[Q:].reshape(width), gains[:Q].reshape(width))


def solution(mesh):
    in_specs = (
        P(("grp", "seq", "dp"), None),
        P(),
        P(("grp", "dp"), "seq", None),
        P(("grp", "dp"), "seq"),
        P(("grp", "dp")),
        P(),
        P(None, None, "seq"),
        P(("grp", "dp"), None, "seq"),
    )
    out_specs = (
        P(("grp", "dp"), None, "seq"),
        P(("grp", "seq", "dp"), None),
        P(None, None, "seq"),
        P(),
        P(),
    )
    return jax.shard_map(local, mesh=mesh, in_specs=in_specs, out_specs=out_specs, check_vma=False)
```

```python
import functools
import math

import jax
import jax.numpy as jnp
from jax import lax
from jax.experimental import pallas as pl
from jax.experimental.pallas import tpu as pltpu
from jax.sharding import PartitionSpec as P

HD = 128
LANES = 128
Q = 8
EPS = 1e-05
MESH = pl.DeviceIdType.MESH
F32, BF16 = jnp.float32, jnp.bfloat16
VMEM_LIMIT = 60 * 2**20


def iota(shape, dim):
    return lax.broadcasted_iota(jnp.int32, shape, dim).astype(F32)


def onehot(mask):
    return jnp.where(mask, 1.0, 0.0).astype(BF16)


def column(row):
    return jnp.broadcast_to(row, (LANES, LANES)).T


def plane_peer(index, nd):
    return {"seq": index // nd, "dp": lax.rem(index, nd)}


def greet(barrier, device):
    pl.semaphore_signal(barrier, inc=1, device_id=device, device_id_type=MESH)


def remote(src, dst, send, recv, device):
    return pltpu.make_async_remote_copy(
        src_ref=src, dst_ref=dst, send_sem=send, recv_sem=recv, device_id=device, device_id_type=MESH
    )


def slots(owner_ref, cap, f):
    own = owner_ref[f].astype(F32)
    length = own.shape[1]
    owner_row = jnp.concatenate([own, own], axis=1)
    owner = jnp.broadcast_to(owner_row, (LANES, LANES))
    this = iota((LANES, LANES), 1)
    this = jnp.where(this >= length, this - length, this)
    earlier = (owner == owner.T) & (iota((LANES, LANES), 0) < this)
    rank_row = jnp.sum(jnp.where(earlier, 1.0, 0.0), axis=0, keepdims=True)
    return owner_row, rank_row, (owner_row * cap + rank_row) * Q


def main_kernel(
    ng, ns, nd, cap,
    count_ref, owner_ref, row_ref, hidden_ref, igain_ref, ugain_ref, weight_ref, dout_ref,
    attn_ref, dhidden_ref, full_ref, ugrad_ref, igrad_ref,
    req, reqr, val, table, out, arr, stack, back_out, back_arr,
    inputs, ufactor, dinputs, uterms,
    gat, prj, dpr, dpt, wgt, part, mix, ring, dk_acc, dv_acc,
    grad_out, gin, tmine, tin, tmid,
    id_send, id_recv, row_send, row_recv, bk_send, bk_recv,
    ag_send, ag_recv, sb_send, sb_recv, mx_send, mx_recv, rs_send, rs_recv,
    gr_send, gr_recv, gg_send, gg_recv, t_send, t_recv, u_send, u_recv,
):
    seqs, _, local_len, width = gat.shape
    items = hidden_ref.shape[0]
    length = ns * local_len
    owners, msg = ns * nd, cap * Q
    per_g = LANES // msg
    groups = owners // per_g
    piece = width // Q
    nr = ng * nd
    nz = ns // 2
    half = nz // 2
    hops = 2 * half - 1
    hl = local_len // 2
    per = 4
    tile = per * local_len
    tiles = ns // per
    seq, dp, grp = lax.axis_index("seq"), lax.axis_index("dp"), lax.axis_index("grp")
    me = seq * nd + dp
    rep = grp * nd + dp
    z, core = seq // 2, lax.rem(seq, 2)
    sib_index = seq + 1 - 2 * core
    sib = {"seq": sib_index}
    ahead = ({"seq": lax.rem(seq + 2, ns)}, {"seq": lax.rem(seq + ns - 2, ns)})
    scale = 1.0 / math.sqrt(HD)
    my_group = me // per_g

    def rep_peer(index):
        return {"grp": index // nd, "dp": lax.rem(index, nd)}

    def turn_of(step):
        turn = (step + 1) // 2 if step % 2 else groups - step // 2
        return lax.rem(my_group + turn, groups)

    barrier = pltpu.get_barrier_semaphore()

    @pl.loop(1, owners)
    def _(i):
        greet(barrier, plane_peer(lax.rem(me + i, owners), nd))

    @pl.loop(nd, nr)
    def _(i):
        greet(barrier, rep_peer(lax.rem(grp * nd + i, nr)))

    lane = lax.broadcasted_iota(jnp.int32, (LANES, LANES), 1)
    slot_in = ((lane % msg) // Q).astype(F32)
    piece_of = (lane[0:1, :] % Q).astype(F32)
    places = []
    for f in range(seqs):
        owner_row, rank_row, base_row = slots(owner_ref, cap, f)
        places.append(base_row)
        want = row_ref[f : f + 1, :].astype(F32) + 1.0
        row_col = column(jnp.concatenate([want, jnp.zeros_like(want)], axis=1))
        wanted = jnp.where(column(rank_row) == slot_in, row_col, 0.0).astype(BF16)
        names = onehot(iota((owners, LANES), 0) == owner_row)
        asked = jnp.dot(names, wanted, preferred_element_type=F32)
        asked = jnp.where(asked > 0.5, asked - 1.0 + piece_of * items, -1.0).astype(jnp.int32)
        for o in range(owners):
            req[o, f : f + 1, :] = asked[o : o + 1, :]

    pl.semaphore_wait(barrier, owners - 1 + nr - nd)

    @pl.loop(1, owners)
    def _(i):
        peer = lax.rem(me + i, owners)
        remote(req.at[peer], reqr.at[me], id_send, id_recv, plane_peer(peer, nd)).start()

    reqr[me] = req[me]
    hidden = hidden_ref[...].astype(F32)
    ifactor = lax.rsqrt(jnp.mean(hidden * hidden, axis=-1, keepdims=True) + EPS)
    for q in range(Q):
        cols = slice(q * piece, (q + 1) * piece)
        table[q * items : (q + 1) * items, :] = (
            hidden_ref[:, cols].astype(F32) * ifactor * igain_ref[:, cols]
        ).astype(BF16)
    remote(
        req.at[pl.ds(0, owners - 1)], reqr.at[pl.ds(0, owners - 1)], id_send, id_recv, plane_peer(me, nd)
    ).wait()

    def send_group(src, dst, f, g, send, recv):
        for k in range(per_g):
            peer = g * per_g + k

            @pl.when(peer != me)
            def _():
                remote(src.at[f, peer], dst.at[f, me], send.at[f], recv.at[f], plane_peer(peer, nd)).start()

    def all_groups(src, dst, f, send, recv):
        some = pl.ds(0, owners - 1)
        return remote(src.at[f, some], dst.at[f, some], send.at[f], recv.at[f], plane_peer(me, nd))

    lane_group = lax.broadcasted_iota(jnp.int32, (1, LANES), 1) // msg

    def fetch(f, step):
        g = turn_of(step)
        ids = jnp.zeros((1, LANES), jnp.int32)
        for k in range(per_g):
            ids = jnp.where(lane_group == k, reqr[g * per_g + k][f : f + 1, :], ids)
        val[f, g] = ids
        col = column(ids.astype(F32))
        pick = jnp.concatenate([onehot(col == iota((LANES, LANES), 1) + q * items) for q in range(Q)], axis=1)
        picked = jnp.dot(pick, table[...], preferred_element_type=F32).astype(BF16)
        out[f, pl.ds(g * per_g, per_g)] = picked.reshape(per_g, msg, piece)
        send_group(out, arr, f, g, row_send, row_recv)

    def place(f):
        arr[f, me] = out[f, me]
        base_col = column(places[f])[0:local_len]
        all_groups(out, arr, f, row_send, row_recv).wait_recv()
        arrived = arr[f].reshape(owners * msg, piece)
        total = jnp.zeros((local_len, 1), F32)
        for q in range(Q):
            put = jnp.concatenate(
                [onehot(iota((local_len, LANES), 1) + t * LANES == base_col + q) for t in range(groups)], axis=1
            )
            rows = jnp.dot(put, arrived, preferred_element_type=F32)
            inputs[f, :, q * piece : (q + 1) * piece] = rows.astype(BF16)
            total += jnp.sum(rows * rows, axis=-1, keepdims=True)
        factor = lax.rsqrt(total / width + EPS)
        ufactor[f] = factor
        gat[f, seq] = (inputs[f].astype(F32) * factor * ugain_ref[...]).astype(BF16)

    def give_back(f, step):
        if step == 0:
            for q in range(Q):
                stack[f, q * local_len : (q + 1) * local_len, :] = dinputs[f, :, q * piece : (q + 1) * piece]
        g = turn_of(step)
        rows = iota((LANES, LANES), 0) + (g * LANES).astype(F32)
        second = jnp.where(iota((1, LANES), 1) >= local_len, 1.0, 0.0)
        put = jnp.concatenate([onehot(rows == places[f] + (2.0 * t + second)) for t in range(Q // 2)], axis=1)
        sent = jnp.dot(put, stack[f], preferred_element_type=F32).astype(BF16)
        back_out[f, pl.ds(g * per_g, per_g)] = sent.reshape(per_g, msg, piece)
        send_group(back_out, back_arr, f, g, bk_send, bk_recv)

    def taken(f):
        back_arr[f, me] = back_out[f, me]
        all_groups(back_out, back_arr, f, bk_send, bk_recv).wait_recv()
        pick = jnp.concatenate([onehot(iota((Q * items, LANES), 0) == val[f, g].astype(F32)) for g in range(groups)], axis=1)
        return jnp.dot(pick, back_arr[f].reshape(owners * msg, piece), preferred_element_type=F32)

    def ag_place(f, d, e, origin):
        far = e // 2
        h = d if e == hops - 1 else e % 2
        block = lax.rem(origin + (ns - 2 * far if d == 0 else 2 * far), ns)
        return gat.at[f, block, pl.ds(h * hl, hl)]

    def ag_copy(f, d, e):
        ref = ag_place(f, d, e, seq)
        return remote(ref, ref, ag_send.at[f, d, e], ag_recv.at[f, d, e], ahead[d])

    def ag_arrival(f, d, e, at):
        behind = lax.rem(at + (ns - 2 if d == 0 else 2), ns)
        return ag_place(f, d, e, behind)

    def ag_wait(f, d, e):
        ref = ag_arrival(f, d, e, seq)
        remote(ref, ref, ag_send.at[f, d, e], ag_recv.at[f, d, e], ahead[d]).wait_recv()

    def sb_copy(f, n):
        ref = gat.at[f, seq] if n == 0 else ag_arrival(f, (n - 1) % 2, (n - 1) // 2, seq)
        return remote(ref, ref, sb_send.at[f, n], sb_recv.at[f, n], sib)

    def sb_wait(f, n):
        ref = gat.at[f, sib_index] if n == 0 else ag_arrival(f, (n - 1) % 2, (n - 1) // 2, sib_index)
        remote(ref, ref, sb_send.at[f, n], sb_recv.at[f, n], sib).wait_recv()

    def ag_begin(f):
        for e in range(min(2, hops)):
            for d in range(2):
                ag_copy(f, d, e).start()
        sb_copy(f, 0).start()

    def ag_event(f, d, e):
        ag_wait(f, d, e)
        if e + 2 < hops - 1:
            ag_copy(f, d, e + 2).start()
        elif e + 2 == hops - 1 + d:
            ag_copy(f, d, hops - 1).start()
        sb_copy(f, 1 + 2 * e + d).start()

    def ag_events(f):
        return [functools.partial(ag_event, f, d, e) for e in range(hops) for d in range(2)]

    def ag_end(f):
        for n in range(1 + 2 * hops):
            sb_wait(f, n)

    order = [(half, None)] + [(t, h) for t in range(half - 1, 0, -1) for h in range(2)]

    def rs_what(d, i):
        t, h = order[i]
        return t, d if h is None else h

    def chip(d, t):
        return lax.rem(z + (t if d == 0 else nz - t), nz)

    def rs_copy(f, d, i):
        t, h = rs_what(d, i)
        return remote(
            mix.at[f, chip(d, t), pl.ds(h * hl, hl)], ring.at[f, d, i], rs_send.at[f, d, i], rs_recv.at[f, d, i], ahead[d]
        )

    def mx_copy(f, k):
        return remote(part.at[f, 2 * k + 1 - core], mix.at[f, k], mx_send.at[f, k], mx_recv.at[f, k], sib)

    def own_sum(f, k):
        mix[f, k] = (mix[f, k].astype(F32) + part[f, 2 * k + core].astype(F32)).astype(BF16)

    def rs_source(d, i):
        t, h = rs_what(d, i)
        for j in range(len(order)):
            if rs_what(d, j) == (t + 1, h):
                return j
        return None

    def rs_own(f, t):
        own_sum(f, chip(0, t))
        if 0 < t < half:
            own_sum(f, chip(1, t))
        for d in range(2):
            for i in range(len(order)):
                if rs_what(d, i)[0] == t and rs_source(d, i) is None:
                    rs_copy(f, d, i).start()

    def rs_start(f):
        for k in range(nz):
            mx_copy(f, k).wait_recv()
        rs_own(f, half)
        rs_own(f, half - 1)

    def rs_event(f, d, j):
        rs_copy(f, d, j).wait_recv()
        t, h = rs_what(d, j)
        if t == 1:
            return
        for i in range(len(order)):
            if rs_what(d, i) == (t - 1, h):
                rows = pl.ds(h * hl, hl)
                k = chip(d, t - 1)
                mix[f, k, rows] = (mix[f, k, rows].astype(F32) + ring[f, d, j].astype(F32)).astype(BF16)
                rs_copy(f, d, i).start()

    def rs_events(f):
        events = [functools.partial(rs_own, f, t) for t in range(half - 2, -1, -1)]
        return events + [functools.partial(rs_event, f, d, j) for j in range(len(order)) for d in range(2)]

    def rs_end(f):
        total = mix[f, z].astype(F32)
        for h in range(2):
            rows = slice(h * hl, (h + 1) * hl)
            got = total[rows]
            for d in range(2):
                for i in range(len(order)):
                    if rs_what(d, i) == (1, h):
                        got = got + ring[f, d, i].astype(F32)
            values = inputs[f, rows, :].astype(F32)
            factor = ufactor[f, rows, :]
            term = jnp.sum(got * values * factor, axis=0, keepdims=True)
            if f == 0 and h == 0:
                uterms[...] = term
            else:
                uterms[...] += term
            weighted = ugain_ref[...] * got
            center = jnp.mean(weighted * values, axis=-1, keepdims=True)
            dinputs[f, rows, :] = (factor * weighted - values * (factor * factor * factor * center)).astype(BF16)

    def project(f, i):
        rows = gat[f, i * per : (i + 1) * per].reshape(tile, width)
        prj[f, i * tile : (i + 1) * tile, :] = jnp.dot(rows, wgt[...], preferred_element_type=F32).astype(BF16)

    def attend(f, i):
        keys_n = (i + 1) * tile
        at = slice(i * tile, (i + 1) * tile)
        query = prj[f, at, 0:HD]
        keys = prj[f, 0:keys_n, HD : 2 * HD]
        values = prj[f, 0:keys_n, 2 * HD : 3 * HD]
        upstream = dout_ref[f, at, :]
        over = (((1,), (1,)), ((), ()))
        down = (((0,), (0,)), ((), ()))
        scores = lax.dot_general(query, keys, over, preferred_element_type=F32) * scale
        p = lax.broadcasted_iota(jnp.int32, (tile, keys_n), 0) + i * tile
        k = lax.broadcasted_iota(jnp.int32, (tile, keys_n), 1)
        allowed = (k <= p) & (k < count_ref[f])
        scores = jnp.where(allowed, scores, -1e30)
        exponent = jnp.exp(scores - jnp.max(scores, axis=-1, keepdims=True))
        weights = exponent * (1.0 / jnp.sum(exponent, axis=-1, keepdims=True))
        weights_b = weights.astype(BF16)
        attn_ref[f, at, :] = jnp.dot(weights_b, values, preferred_element_type=F32).astype(BF16)
        d_weights = lax.dot_general(upstream, values, over, preferred_element_type=F32)
        center = jnp.sum(weights * d_weights, axis=-1, keepdims=True)
        d_scores = (weights * (d_weights - center) * scale).astype(BF16)
        dpr[f, at, 0:HD] = jnp.dot(d_scores, keys, preferred_element_type=F32).astype(BF16)
        d_values = lax.dot_general(weights_b, upstream, down, preferred_element_type=F32)
        d_keys = lax.dot_general(d_scores, query, down, preferred_element_type=F32)
        old = i * tile
        if i:
            dv_acc[0:old, :] += d_values[0:old]
            dk_acc[0:old, :] += d_keys[0:old]
        dv_acc[at, :] = d_values[old:]
        dk_acc[at, :] = d_keys[old:]

    def attended(f):
        dpr[f, :, HD : 2 * HD] = dk_acc[...].astype(BF16)
        dpr[f, :, 2 * HD : 3 * HD] = dv_acc[...].astype(BF16)

    def back(f, i):
        rows = dpr[f, i * tile : (i + 1) * tile, :]
        term = lax.dot_general(rows, wgt[...], (((1,), (1,)), ((), ())), preferred_element_type=F32)
        part[f, i * per : (i + 1) * per] = term.astype(BF16).reshape(per, local_len, width)
        for k in range(per // 2):
            mx_copy(f, i * per // 2 + k).start()

    def turned(f):
        dpt[:, f * length : (f + 1) * length] = dpr[f].T

    def grad(j):
        cols = slice(j * 2 * LANES, (j + 1) * 2 * LANES)
        got = jnp.zeros((dpt.shape[0], 2 * LANES), F32)
        for f in range(seqs):
            rows = gat[f, :, :, cols].reshape(length, 2 * LANES)
            got += jnp.dot(dpt[:, f * length : (f + 1) * length], rows, preferred_element_type=F32)
        for k in range(2):
            grad_out[2 * j + k] = got[:, k * LANES : (k + 1) * LANES].astype(BF16)

    gchunk = width // LANES // nr
    gmine = pl.ds(rep * gchunk, gchunk)
    gsome = pl.ds(0, (nr - 1) * gchunk)

    def grads_start():
        @pl.loop(1, nr)
        def _(i):
            peer = lax.rem(rep + i, nr)
            remote(grad_out.at[pl.ds(peer * gchunk, gchunk)], gin.at[rep], gr_send, gr_recv, rep_peer(peer)).start()

        gin[rep] = grad_out[gmine]

    def grads_sum():
        remote(grad_out.at[gsome], grad_out.at[gsome], gr_send, gr_recv, rep_peer(rep)).wait_recv()
        got = gin[0].astype(F32)
        for i in range(1, nr):
            got += gin[i].astype(F32)
        full_ref[gmine] = got.astype(BF16)

        @pl.loop(1, nr)
        def _(i):
            remote(full_ref.at[gmine], full_ref.at[gmine], gg_send, gg_recv, rep_peer(lax.rem(rep + i, nr))).start()

    def gain_start(n):
        tin[n, seq] = tmine[n]

        @pl.loop(1, ns)
        def _(i):
            remote(tmine.at[n], tin.at[n, seq], t_send.at[n], t_recv.at[n], {"seq": lax.rem(seq + i, ns)}).start()

    def gain_turn(n):
        some = pl.ds(0, ns - 1)
        remote(tin.at[n, some], tin.at[n, some], t_send.at[n], t_recv.at[n], {"seq": seq}).wait()
        total = tin[n, 0]
        for i in range(1, ns):
            total = total + tin[n, i]
        tmid[n, rep] = total

        @pl.loop(1, nr)
        def _(i):
            there = tmid.at[n, rep]
            remote(there, there, u_send.at[n], u_recv.at[n], rep_peer(lax.rem(rep + i, nr))).start()

    def gain_end(n, to_ref):
        some = pl.ds(0, nr - 1)
        remote(tmid.at[n, some], tmid.at[n, some], u_send.at[n], u_recv.at[n], rep_peer(rep)).wait()
        total = tmid[n, 0]
        for i in range(1, nr):
            total = total + tmid[n, i]
        for q in range(Q):
            to_ref[:, q * piece : (q + 1) * piece] = total[q : q + 1, :]

    def sequence_work(f):
        work = [functools.partial(project, f, i) for i in range(tiles)]
        work += [functools.partial(attend, f, i) for i in range(tiles)]
        work += [functools.partial(attended, f)]
        return work + [functools.partial(back, f, i) for i in range(tiles)]

    def interleave(events, work):
        done = 0
        for n, event in enumerate(events):
            event()
            upto = (n + 1) * len(work) // len(events)
            for item in work[done:upto]:
                item()
            done = upto

    for f in range(seqs):
        for step in range(groups):
            fetch(f, step)
    for c in range(3):
        wgt[:, c * HD : (c + 1) * HD] = weight_ref[c]
    place(0)
    ag_begin(0)
    events = ag_events(0)
    first, last = 2 * hops // 4, 2 * hops // 2
    interleave(events[:first], [])
    place(1)
    interleave(events[first:last], [])
    ag_begin(1)
    interleave(events[last:], [])
    ag_end(0)
    events = ag_events(1)
    interleave(events[:-4], sequence_work(0))
    rs_start(0)
    interleave(events[-4:], [])
    ag_end(1)
    events = rs_events(0)
    interleave(events[:-4], [functools.partial(turned, 0)] + sequence_work(1))
    rs_start(1)
    interleave(events[-4:], [])
    rs_end(0)
    work = [functools.partial(turned, 1)] + [functools.partial(grad, j) for j in range(width // (2 * LANES))]
    work += [grads_start] + [functools.partial(give_back, 0, step) for step in range(groups)]
    interleave(rs_events(1), work)
    rs_end(1)
    for step in range(groups):
        give_back(1, step)
    for q in range(Q):
        tmine[0, q : q + 1, :] = uterms[:, q * piece : (q + 1) * piece]
    gain_start(0)
    grads_sum()
    gain_turn(0)
    took = taken(0)
    gain_end(0, ugrad_ref)
    took = took + taken(1)
    center = jnp.zeros((items, 1), F32)
    for q in range(Q):
        cols = slice(q * piece, (q + 1) * piece)
        h = hidden_ref[:, cols].astype(F32)
        d = took[q * items : (q + 1) * items]
        center += jnp.sum(igain_ref[:, cols] * d * h, axis=-1, keepdims=True)
        tmine[1, q : q + 1, :] = jnp.sum(d * h * ifactor, axis=0, keepdims=True)
    center = center / width
    gain_start(1)
    for q in range(Q):
        cols = slice(q * piece, (q + 1) * piece)
        h = hidden_ref[:, cols].astype(F32)
        d = took[q * items : (q + 1) * items]
        dhidden_ref[:, cols] = (
            ifactor * igain_ref[:, cols] * d - h * (ifactor * ifactor * ifactor * center)
        ).astype(BF16)
    gain_turn(1)
    for f in range(seqs):
        all_groups(out, arr, f, row_send, row_recv).wait_send()
        all_groups(back_out, back_arr, f, bk_send, bk_recv).wait_send()
        for d in range(2):
            for e in range(hops):
                ag_copy(f, d, e).wait_send()
                rs_copy(f, d, e).wait_send()
        for n in range(1 + 2 * hops):
            sb_copy(f, n).wait_send()
        for k in range(nz):
            mx_copy(f, k).wait_send()
    remote(grad_out.at[gsome], grad_out.at[gsome], gr_send, gr_recv, rep_peer(rep)).wait_send()
    remote(full_ref.at[gsome], full_ref.at[gsome], gg_send, gg_recv, rep_peer(rep)).wait()
    gain_end(1, igrad_ref)


def main(ng, ns, nd, cap, count, owner, row, hidden, igain, ugain, weight, dout):
    items, width = hidden.shape
    seqs, local_len = row.shape
    length = ns * local_len
    owners, msg = ns * nd, cap * Q
    piece = width // Q
    nr, nz = ng * nd, ns // 2
    hops = nz - 1
    cols = 3 * HD
    vmem = pl.BlockSpec(memory_space=pltpu.VMEM)
    full = (width // LANES, cols, LANES)
    dma = pltpu.SemaphoreType.DMA
    return pl.pallas_call(
        functools.partial(main_kernel, ng, ns, nd, cap),
        out_shape=(
            jax.ShapeDtypeStruct((seqs, length, HD), BF16),
            jax.ShapeDtypeStruct((items, width), BF16),
            jax.ShapeDtypeStruct(full, BF16),
            jax.ShapeDtypeStruct((1, width), F32),
            jax.ShapeDtypeStruct((1, width), F32),
        ),
        in_specs=[pl.BlockSpec(memory_space=pltpu.SMEM)] + [vmem] * 7,
        out_specs=[vmem] * 5,
        scratch_shapes=[
            pltpu.VMEM((owners, seqs, LANES), jnp.int32),
            pltpu.VMEM((owners, seqs, LANES), jnp.int32),
            pltpu.VMEM((seqs, owners * msg // LANES, 1, LANES), jnp.int32),
            pltpu.VMEM((Q * items, piece), BF16),
            pltpu.VMEM((seqs, owners, msg, piece), BF16),
            pltpu.VMEM((seqs, owners, msg, piece), BF16),
            pltpu.VMEM((seqs, Q * local_len, piece), BF16),
            pltpu.VMEM((seqs, owners, msg, piece), BF16),
            pltpu.VMEM((seqs, owners, msg, piece), BF16),
            pltpu.VMEM((seqs, local_len, width), BF16),
            pltpu.VMEM((seqs, local_len, 1), F32),
            pltpu.VMEM((seqs, local_len, width), BF16),
            pltpu.VMEM((1, width), F32),
            pltpu.VMEM((seqs, ns, local_len, width), BF16),
            pltpu.VMEM((seqs, length, cols), BF16),
            pltpu.VMEM((seqs, length, cols), BF16),
            pltpu.VMEM((cols, seqs * length), BF16),
            pltpu.VMEM((width, cols), BF16),
            pltpu.VMEM((seqs, ns, local_len, width), BF16),
            pltpu.VMEM((seqs, nz, local_len, width), BF16),
            pltpu.VMEM((seqs, 2, hops, local_len // 2, width), BF16),
            pltpu.VMEM((length, HD), F32),
            pltpu.VMEM((length, HD), F32),
            pltpu.VMEM(full, BF16),
            pltpu.VMEM((nr, full[0] // nr, cols, LANES), BF16),
            pltpu.VMEM((2, Q, piece), F32),
            pltpu.VMEM((2, ns, Q, piece), F32),
            pltpu.VMEM((2, nr, Q, piece), F32),
        ]
        + [dma] * 2
        + [dma((seqs,))] * 4
        + [dma((seqs, 2, hops))] * 2
        + [dma((seqs, 1 + 2 * hops))] * 2
        + [dma((seqs, nz))] * 2
        + [dma((seqs, 2, hops))] * 2
        + [dma] * 4
        + [dma((2,))] * 4,
        compiler_params=pltpu.CompilerParams(
            collective_id=0, has_side_effects=True, vmem_limit_bytes=VMEM_LIMIT
        ),
        name="main",
    )(count, owner, row, hidden, igain, ugain, weight, dout)


def finish_kernel(attn_in, dhidden_in, full_ref, ugrad_in, igrad_in, attn_ref, dhidden_ref, grad_ref, ugrad_ref, igrad_ref, sems):
    step = pl.program_id(0)

    def copies():
        pairs = ((attn_in, attn_ref), (dhidden_in, dhidden_ref), (ugrad_in, ugrad_ref), (igrad_in, igrad_ref))
        return [pltpu.make_async_copy(a, b, sems.at[n]) for n, (a, b) in enumerate(pairs)]

    @pl.when(step == 0)
    def _():
        for copy in copies():
            copy.start()

    for i in range(full_ref.shape[0]):
        grad_ref[0, i * LANES : (i + 1) * LANES, :] = full_ref[i].astype(F32).T

    @pl.when(step == pl.num_programs(0) - 1)
    def _():
        for copy in copies():
            copy.wait()


def finish(attn, dhidden, full, ugrad, igrad):
    chunks = full.shape[0]
    width = chunks * LANES
    anyspace = pl.BlockSpec(memory_space=pl.ANY)
    return pl.pallas_call(
        finish_kernel,
        grid=(3,),
        out_shape=(
            jax.ShapeDtypeStruct(attn.shape, BF16),
            jax.ShapeDtypeStruct(dhidden.shape, BF16),
            jax.ShapeDtypeStruct((3, width, HD), F32),
            jax.ShapeDtypeStruct(ugrad.shape, F32),
            jax.ShapeDtypeStruct(igrad.shape, F32),
        ),
        in_specs=[anyspace, anyspace, pl.BlockSpec((chunks, HD, LANES), lambda c: (0, c, 0)), anyspace, anyspace],
        out_specs=[anyspace, anyspace, pl.BlockSpec((1, width, HD), lambda c: (c, 0, 0)), anyspace, anyspace],
        scratch_shapes=[pltpu.SemaphoreType.DMA((4,))],
        name="finish",
    )(attn, dhidden, full, ugrad, igrad)


def local(
    item_hidden, item_gain, slot_owner, slot_row, seq_count, user_gain, query_key_value_weight, d_out
):
    ng, ns, nd = (lax.axis_size(a) for a in ("grp", "seq", "dp"))
    seqs, local_len, _ = slot_owner.shape
    width = item_hidden.shape[1]
    cap = max(2, 2 * local_len // (ns * nd))
    igain, ugain = item_gain.reshape(1, width), user_gain.reshape(1, width)
    owner = slot_owner.transpose(0, 2, 1)
    attn, d_hidden, full, ugrad, igrad = main(
        ng, ns, nd, cap, seq_count, owner, slot_row, item_hidden, igain, ugain, query_key_value_weight, d_out
    )
    attn, d_hidden, grads, ugrad, igrad = finish(attn, d_hidden, full, ugrad, igrad)
    return (attn, d_hidden, grads, ugrad.reshape(width), igrad.reshape(width))


def solution(mesh):
    in_specs = (
        P(("grp", "seq", "dp"), None),
        P(),
        P(("grp", "dp"), "seq", None),
        P(("grp", "dp"), "seq"),
        P(("grp", "dp")),
        P(),
        P(None, None, "seq"),
        P(("grp", "dp"), None, "seq"),
    )
    out_specs = (
        P(("grp", "dp"), None, "seq"),
        P(("grp", "seq", "dp"), None),
        P(None, None, "seq"),
        P(),
        P(),
    )
    return jax.shard_map(local, mesh=mesh, in_specs=in_specs, out_specs=out_specs, check_vma=False)
```

```python
import functools
import math

import jax
import jax.numpy as jnp
from jax import lax
from jax.experimental import pallas as pl
from jax.experimental.pallas import tpu as pltpu
from jax.sharding import PartitionSpec as P

HD = 128
LANES = 128
Q = 8
EPS = 1e-05
MESH = pl.DeviceIdType.MESH
F32, BF16 = jnp.float32, jnp.bfloat16
VMEM_LIMIT = 60 * 2**20


def iota(shape, dim):
    return lax.broadcasted_iota(jnp.int32, shape, dim).astype(F32)


def onehot(mask):
    return jnp.where(mask, 1.0, 0.0).astype(BF16)


def column(row):
    return jnp.broadcast_to(row, (LANES, LANES)).T


def plane_peer(index, nd):
    return {"seq": index // nd, "dp": lax.rem(index, nd)}


def greet(barrier, device):
    pl.semaphore_signal(barrier, inc=1, device_id=device, device_id_type=MESH)


def remote(src, dst, send, recv, device):
    return pltpu.make_async_remote_copy(
        src_ref=src, dst_ref=dst, send_sem=send, recv_sem=recv, device_id=device, device_id_type=MESH
    )


def slots(owner_ref, cap, f):
    own = owner_ref[f].astype(F32)
    length = own.shape[1]
    owner_row = jnp.concatenate([own, own], axis=1)
    owner = jnp.broadcast_to(owner_row, (LANES, LANES))
    this = iota((LANES, LANES), 1)
    this = jnp.where(this >= length, this - length, this)
    earlier = (owner == owner.T) & (iota((LANES, LANES), 0) < this)
    rank_row = jnp.sum(jnp.where(earlier, 1.0, 0.0), axis=0, keepdims=True)
    return owner_row, rank_row, (owner_row * cap + rank_row) * Q


def main_kernel(
    ng, ns, nd, cap,
    count_ref, owner_ref, row_ref, hidden_ref, igain_ref, ugain_ref, weight_in, dout_in,
    attn_ref, dhidden_ref, full_ref, ugrad_ref, igrad_ref,
    req, reqr, val, table, out, arr, stack, back_out, back_arr,
    inputs, ufactor, dinputs, uterms,
    gat, prj, dpr, dpt, wgt, part, mix, ring, dk_acc, dv_acc,
    grad_out, gin, tmine, tin, tmid, tall, picks, iterms, weight_ref, dout_ref, load_sem,
    id_send, id_recv, row_send, row_recv, bk_send, bk_recv,
    ag_send, ag_recv, sb_send, sb_recv, mx_send, mx_recv, rs_send, rs_recv,
    gr_send, gr_recv, gg_send, gg_recv, t_send, t_recv, u_send, u_recv, v_send, v_recv,
):
    seqs, _, local_len, width = gat.shape
    items = hidden_ref.shape[0]
    length = ns * local_len
    owners, msg = ns * nd, cap * Q
    per_g = LANES // msg
    groups = owners // per_g
    piece = width // Q
    nr = ng * nd
    nz = ns // 2
    half = nz // 2
    hops = 2 * half - 1
    hl = local_len // 2
    per = 4
    tile = per * local_len
    tiles = ns // per
    seq, dp, grp = lax.axis_index("seq"), lax.axis_index("dp"), lax.axis_index("grp")
    me = seq * nd + dp
    rep = grp * nd + dp
    z, core = seq // 2, lax.rem(seq, 2)
    sib_index = seq + 1 - 2 * core
    sib = {"seq": sib_index}
    ahead = ({"seq": lax.rem(seq + 2, ns)}, {"seq": lax.rem(seq + ns - 2, ns)})
    scale = 1.0 / math.sqrt(HD)
    my_group = me // per_g

    def rep_peer(index):
        return {"grp": index // nd, "dp": lax.rem(index, nd)}

    def turn_of(step):
        far = groups // 2 - (step + 1) // 2
        return lax.rem(my_group + (far if step % 2 == 0 else groups - far), groups)

    barrier = pltpu.get_barrier_semaphore()
    loads = (
        pltpu.make_async_copy(weight_in, weight_ref, load_sem.at[0]),
        pltpu.make_async_copy(dout_in, dout_ref, load_sem.at[1]),
    )
    for load in loads:
        load.start()

    @pl.loop(1, owners)
    def _(i):
        greet(barrier, plane_peer(lax.rem(me + i, owners), nd))

    @pl.loop(nd, nr)
    def _(i):
        greet(barrier, rep_peer(lax.rem(grp * nd + i, nr)))

    lane = lax.broadcasted_iota(jnp.int32, (LANES, LANES), 1)
    slot_in = ((lane % msg) // Q).astype(F32)
    piece_of = (lane[0:1, :] % Q).astype(F32)
    places = []
    for f in range(seqs):
        owner_row, rank_row, base_row = slots(owner_ref, cap, f)
        places.append(base_row)
        want = row_ref[f : f + 1, :].astype(F32) + 1.0
        row_col = column(jnp.concatenate([want, jnp.zeros_like(want)], axis=1))
        wanted = jnp.where(column(rank_row) == slot_in, row_col, 0.0).astype(BF16)
        names = onehot(iota((owners, LANES), 0) == owner_row)
        asked = jnp.dot(names, wanted, preferred_element_type=F32)
        asked = jnp.where(asked > 0.5, asked - 1.0 + piece_of * items, -1.0).astype(jnp.int32)
        for o in range(owners):
            req[o, f : f + 1, :] = asked[o : o + 1, :]

    pl.semaphore_wait(barrier, owners - 1 + nr - nd)

    @pl.loop(1, owners)
    def _(i):
        peer = lax.rem(me + i, owners)
        remote(req.at[peer], reqr.at[me], id_send, id_recv, plane_peer(peer, nd)).start()

    reqr[me] = req[me]
    hidden = hidden_ref[...].astype(F32)
    ifactor = lax.rsqrt(jnp.mean(hidden * hidden, axis=-1, keepdims=True) + EPS)
    for q in range(Q):
        cols = slice(q * piece, (q + 1) * piece)
        table[q * items : (q + 1) * items, :] = (
            hidden_ref[:, cols].astype(F32) * ifactor * igain_ref[:, cols]
        ).astype(BF16)
    remote(
        req.at[pl.ds(0, owners - 1)], reqr.at[pl.ds(0, owners - 1)], id_send, id_recv, plane_peer(me, nd)
    ).wait()

    def send_group(src, dst, f, g, send, recv):
        for k in range(per_g):
            peer = g * per_g + k

            @pl.when(peer != me)
            def _():
                remote(src.at[f, peer], dst.at[f, me], send.at[f], recv.at[f], plane_peer(peer, nd)).start()

    def all_groups(src, dst, f, send, recv):
        some = pl.ds(0, owners - 1)
        return remote(src.at[f, some], dst.at[f, some], send.at[f], recv.at[f], plane_peer(me, nd))

    lane_group = lax.broadcasted_iota(jnp.int32, (1, LANES), 1) // msg

    def fetch(f, step):
        g = turn_of(step)
        ids = jnp.zeros((1, LANES), jnp.int32)
        for k in range(per_g):
            ids = jnp.where(lane_group == k, reqr[g * per_g + k][f : f + 1, :], ids)
        val[f, g] = ids
        col = column(ids.astype(F32))
        pick = jnp.concatenate([onehot(col == iota((LANES, LANES), 1) + q * items) for q in range(Q)], axis=1)
        picked = jnp.dot(pick, table[...], preferred_element_type=F32).astype(BF16)
        out[f, pl.ds(g * per_g, per_g)] = picked.reshape(per_g, msg, piece)
        send_group(out, arr, f, g, row_send, row_recv)

    def place(f):
        arr[f, me] = out[f, me]
        base_col = column(places[f])[0:local_len]
        all_groups(out, arr, f, row_send, row_recv).wait_recv()
        arrived = arr[f].reshape(owners * msg, piece)
        total = jnp.zeros((local_len, 1), F32)
        for q in range(Q):
            put = jnp.concatenate(
                [onehot(iota((local_len, LANES), 1) + t * LANES == base_col + q) for t in range(groups)], axis=1
            )
            rows = jnp.dot(put, arrived, preferred_element_type=F32)
            inputs[f, :, q * piece : (q + 1) * piece] = rows.astype(BF16)
            total += jnp.sum(rows * rows, axis=-1, keepdims=True)
        factor = lax.rsqrt(total / width + EPS)
        ufactor[f] = factor
        gat[f, seq] = (inputs[f].astype(F32) * factor * ugain_ref[...]).astype(BF16)

    def give_back(f, step):
        if step == 0:
            for q in range(Q):
                stack[f, q * local_len : (q + 1) * local_len, :] = dinputs[f, :, q * piece : (q + 1) * piece]
        g = turn_of(step)
        rows = iota((LANES, LANES), 0) + (g * LANES).astype(F32)
        second = jnp.where(iota((1, LANES), 1) >= local_len, 1.0, 0.0)
        put = jnp.concatenate([onehot(rows == places[f] + (2.0 * t + second)) for t in range(Q // 2)], axis=1)
        sent = jnp.dot(put, stack[f], preferred_element_type=F32).astype(BF16)
        back_out[f, pl.ds(g * per_g, per_g)] = sent.reshape(per_g, msg, piece)
        send_group(back_out, back_arr, f, g, bk_send, bk_recv)

    def taken(f):
        back_arr[f, me] = back_out[f, me]
        for g in range(groups):
            picks[:, g * LANES : (g + 1) * LANES] = onehot(iota((Q * items, LANES), 0) == val[f, g].astype(F32))
        all_groups(back_out, back_arr, f, bk_send, bk_recv).wait_recv()
        return jnp.dot(picks[...], back_arr[f].reshape(owners * msg, piece), preferred_element_type=F32)

    def ag_place(f, d, e, origin):
        far = e // 2
        h = d if e == hops - 1 else e % 2
        block = lax.rem(origin + (ns - 2 * far if d == 0 else 2 * far), ns)
        return gat.at[f, block, pl.ds(h * hl, hl)]

    def ag_copy(f, d, e):
        ref = ag_place(f, d, e, seq)
        return remote(ref, ref, ag_send.at[f, d, e], ag_recv.at[f, d, e], ahead[d])

    def ag_arrival(f, d, e, at):
        behind = lax.rem(at + (ns - 2 if d == 0 else 2), ns)
        return ag_place(f, d, e, behind)

    def ag_wait(f, d, e):
        ref = ag_arrival(f, d, e, seq)
        remote(ref, ref, ag_send.at[f, d, e], ag_recv.at[f, d, e], ahead[d]).wait_recv()

    def sb_copy(f, n):
        ref = gat.at[f, seq] if n == 0 else ag_arrival(f, (n - 1) % 2, (n - 1) // 2, seq)
        return remote(ref, ref, sb_send.at[f, n], sb_recv.at[f, n], sib)

    def sb_wait(f, n):
        ref = gat.at[f, sib_index] if n == 0 else ag_arrival(f, (n - 1) % 2, (n - 1) // 2, sib_index)
        remote(ref, ref, sb_send.at[f, n], sb_recv.at[f, n], sib).wait_recv()

    def ag_begin(f):
        for e in range(min(2, hops)):
            for d in range(2):
                ag_copy(f, d, e).start()
        sb_copy(f, 0).start()

    def ag_event(f, d, e):
        ag_wait(f, d, e)
        if e + 2 < hops - 1:
            ag_copy(f, d, e + 2).start()
        elif e + 2 == hops - 1 + d:
            ag_copy(f, d, hops - 1).start()
        sb_copy(f, 1 + 2 * e + d).start()

    def ag_events(f):
        return [functools.partial(ag_event, f, d, e) for e in range(hops) for d in range(2)]

    def ag_end(f):
        for n in range(1 + 2 * hops):
            sb_wait(f, n)

    order = [(half, None)] + [(t, h) for t in range(half - 1, 0, -1) for h in range(2)]

    def rs_what(d, i):
        t, h = order[i]
        return t, d if h is None else h

    def chip(d, t):
        return lax.rem(z + (t if d == 0 else nz - t), nz)

    def rs_copy(f, d, i):
        t, h = rs_what(d, i)
        return remote(
            mix.at[f, chip(d, t), pl.ds(h * hl, hl)], ring.at[f, d, i], rs_send.at[f, d, i], rs_recv.at[f, d, i], ahead[d]
        )

    def mx_copy(f, k):
        return remote(part.at[f, 2 * k + 1 - core], mix.at[f, k], mx_send.at[f, k], mx_recv.at[f, k], sib)

    def own_sum(f, k):
        mix[f, k] = (mix[f, k].astype(F32) + part[f, 2 * k + core].astype(F32)).astype(BF16)

    def rs_source(d, i):
        t, h = rs_what(d, i)
        for j in range(len(order)):
            if rs_what(d, j) == (t + 1, h):
                return j
        return None

    def rs_own(f, t):
        own_sum(f, chip(0, t))
        if 0 < t < half:
            own_sum(f, chip(1, t))
        for d in range(2):
            for i in range(len(order)):
                if rs_what(d, i)[0] == t and rs_source(d, i) is None:
                    rs_copy(f, d, i).start()

    def rs_start(f):
        for k in range(nz):
            mx_copy(f, k).wait_recv()
        rs_own(f, half)
        rs_own(f, half - 1)

    def rs_event(f, d, j):
        rs_copy(f, d, j).wait_recv()
        t, h = rs_what(d, j)
        if t == 1:
            return
        for i in range(len(order)):
            if rs_what(d, i) == (t - 1, h):
                rows = pl.ds(h * hl, hl)
                k = chip(d, t - 1)
                mix[f, k, rows] = (mix[f, k, rows].astype(F32) + ring[f, d, j].astype(F32)).astype(BF16)
                rs_copy(f, d, i).start()

    def rs_events(f):
        events = [functools.partial(rs_own, f, t) for t in range(half - 2, -1, -1)]
        return events + [functools.partial(rs_event, f, d, j) for j in range(len(order)) for d in range(2)]

    def rs_end(f):
        total = mix[f, z].astype(F32)
        for h in range(2):
            rows = slice(h * hl, (h + 1) * hl)
            got = total[rows]
            for d in range(2):
                for i in range(len(order)):
                    if rs_what(d, i) == (1, h):
                        got = got + ring[f, d, i].astype(F32)
            values = inputs[f, rows, :].astype(F32)
            factor = ufactor[f, rows, :]
            weighted = ugain_ref[...] * got
            center = jnp.mean(weighted * values, axis=-1, keepdims=True)
            d_in = factor * weighted - values * (factor * factor * factor * center)
            dinputs[f, rows, :] = d_in.astype(BF16)
            for ref, term in ((uterms, got * values * factor), (iterms, d_in * values)):
                term = jnp.sum(term, axis=0, keepdims=True)
                if f == 0 and h == 0:
                    ref[...] = term
                else:
                    ref[...] += term

    def project(f, i):
        rows = gat[f, i * per : (i + 1) * per].reshape(tile, width)
        prj[f, i * tile : (i + 1) * tile, :] = jnp.dot(rows, wgt[...], preferred_element_type=F32).astype(BF16)

    def attend(f, i):
        keys_n = (i + 1) * tile
        at = slice(i * tile, (i + 1) * tile)
        query = prj[f, at, 0:HD]
        keys = prj[f, 0:keys_n, HD : 2 * HD]
        values = prj[f, 0:keys_n, 2 * HD : 3 * HD]
        upstream = dout_ref[f, at, :]
        over = (((1,), (1,)), ((), ()))
        down = (((0,), (0,)), ((), ()))
        scores = lax.dot_general(query, keys, over, preferred_element_type=F32) * scale
        p = lax.broadcasted_iota(jnp.int32, (tile, keys_n), 0) + i * tile
        k = lax.broadcasted_iota(jnp.int32, (tile, keys_n), 1)
        allowed = (k <= p) & (k < count_ref[f])
        scores = jnp.where(allowed, scores, -1e30)
        exponent = jnp.exp(scores - jnp.max(scores, axis=-1, keepdims=True))
        weights = exponent * (1.0 / jnp.sum(exponent, axis=-1, keepdims=True))
        weights_b = weights.astype(BF16)
        attn_ref[f, at, :] = jnp.dot(weights_b, values, preferred_element_type=F32).astype(BF16)
        d_weights = lax.dot_general(upstream, values, over, preferred_element_type=F32)
        center = jnp.sum(weights * d_weights, axis=-1, keepdims=True)
        d_scores = (weights * (d_weights - center) * scale).astype(BF16)
        dpr[f, at, 0:HD] = jnp.dot(d_scores, keys, preferred_element_type=F32).astype(BF16)
        d_values = lax.dot_general(weights_b, upstream, down, preferred_element_type=F32)
        d_keys = lax.dot_general(d_scores, query, down, preferred_element_type=F32)
        old = i * tile
        if i:
            dv_acc[0:old, :] += d_values[0:old]
            dk_acc[0:old, :] += d_keys[0:old]
        dv_acc[at, :] = d_values[old:]
        dk_acc[at, :] = d_keys[old:]

    def attended(f):
        dpr[f, :, HD : 2 * HD] = dk_acc[...].astype(BF16)
        dpr[f, :, 2 * HD : 3 * HD] = dv_acc[...].astype(BF16)

    def back(f, i):
        rows = dpr[f, i * tile : (i + 1) * tile, :]
        term = lax.dot_general(rows, wgt[...], (((1,), (1,)), ((), ())), preferred_element_type=F32)
        part[f, i * per : (i + 1) * per] = term.astype(BF16).reshape(per, local_len, width)
        for k in range(per // 2):
            mx_copy(f, i * per // 2 + k).start()

    def turned(f):
        dpt[:, f * length : (f + 1) * length] = dpr[f].T

    def grad(j):
        cols = slice(j * 2 * LANES, (j + 1) * 2 * LANES)
        got = jnp.zeros((dpt.shape[0], 2 * LANES), F32)
        for f in range(seqs):
            rows = gat[f, :, :, cols].reshape(length, 2 * LANES)
            got += jnp.dot(dpt[:, f * length : (f + 1) * length], rows, preferred_element_type=F32)
        for k in range(2):
            grad_out[2 * j + k] = got[:, k * LANES : (k + 1) * LANES].astype(BF16)

    gchunk = width // LANES // nr
    gmine = pl.ds(rep * gchunk, gchunk)
    gsome = pl.ds(0, (nr - 1) * gchunk)

    away = sorted(
        ((a, b) for a in range(ng) for b in range(nd) if a or b),
        key=lambda o: (min(o[0], ng - o[0]) + min(o[1], nd - o[1]), (o[0] + 2 * o[1]) % 3, o),
    )

    def rep_at(a, b):
        return lax.rem(grp + a, ng) * nd + lax.rem(dp + b, nd)

    def grads_start():
        for a, b in away:
            peer = rep_at(a, b)
            remote(grad_out.at[pl.ds(peer * gchunk, gchunk)], gin.at[rep], gr_send, gr_recv, rep_peer(peer)).start()

        gin[rep] = grad_out[gmine]

    def grads_sum():
        remote(grad_out.at[gsome], grad_out.at[gsome], gr_send, gr_recv, rep_peer(rep)).wait_recv()
        got = gin[0].astype(F32)
        for i in range(1, nr):
            got += gin[i].astype(F32)
        full_ref[gmine] = got.astype(BF16)

        for a, b in away:
            remote(full_ref.at[gmine], full_ref.at[gmine], gg_send, gg_recv, rep_peer(rep_at(a, b))).start()

    rp = 2 * Q // ns
    tsome = pl.ds(0, ns - 1)

    def gain_start():
        for q in range(Q):
            cols = slice(q * piece, (q + 1) * piece)
            tmine[q] = iterms[:, cols] / igain_ref[:, cols]
            tmine[Q + q] = uterms[:, cols]

        @pl.loop(1, ns)
        def _(i):
            peer = lax.rem(seq + i, ns)
            remote(tmine.at[pl.ds(peer * rp, rp)], tin.at[seq], t_send, t_recv, {"seq": peer}).start()

        tin[seq] = tmine[pl.ds(seq * rp, rp)]

    def gain_turn():
        remote(tin.at[tsome], tin.at[tsome], t_send, t_recv, {"seq": seq}).wait()
        total = tin[0]
        for i in range(1, ns):
            total = total + tin[i]
        tmid[rep] = total
        for a, b in away:
            remote(tmid.at[rep], tmid.at[rep], u_send, u_recv, rep_peer(rep_at(a, b))).start()

    def gain_spread():
        some = pl.ds(0, nr - 1)
        remote(tmid.at[some], tmid.at[some], u_send, u_recv, rep_peer(rep)).wait()
        total = tmid[0]
        for i in range(1, nr):
            total = total + tmid[i]
        mine = pl.ds(seq * rp, rp)
        tall[mine] = total

        @pl.loop(1, ns)
        def _(i):
            remote(tall.at[mine], tall.at[mine], v_send, v_recv, {"seq": lax.rem(seq + i, ns)}).start()

    def gain_end():
        some = pl.ds(0, (ns - 1) * rp)
        remote(tall.at[some], tall.at[some], v_send, v_recv, {"seq": seq}).wait()
        for q in range(Q):
            cols = slice(q * piece, (q + 1) * piece)
            igrad_ref[:, cols] = tall[q]
            ugrad_ref[:, cols] = tall[Q + q]

    def sequence_work(f):
        work = [functools.partial(project, f, i) for i in range(tiles)]
        work += [functools.partial(attend, f, i) for i in range(tiles)]
        work += [functools.partial(attended, f)]
        return work + [functools.partial(back, f, i) for i in range(tiles)]

    def interleave(events, work):
        done = 0
        for n, event in enumerate(events):
            event()
            upto = (n + 1) * len(work) // len(events)
            for item in work[done:upto]:
                item()
            done = upto

    for f in range(seqs):
        for step in range(groups):
            fetch(f, step)
    for load in loads:
        load.wait()
    for c in range(3):
        wgt[:, c * HD : (c + 1) * HD] = weight_ref[c]
    place(0)
    ag_begin(0)
    events = ag_events(0)
    first, last = 2 * hops // 4, 2 * hops // 2
    interleave(events[:first], [])
    place(1)
    interleave(events[first:last], [])
    ag_begin(1)
    interleave(events[last:], [])
    ag_end(0)
    events = ag_events(1)
    interleave(events[:-4], sequence_work(0))
    rs_start(0)
    interleave(events[-4:], [])
    ag_end(1)
    events = rs_events(0)
    interleave(events[:-4], [functools.partial(turned, 0)] + sequence_work(1))
    rs_start(1)
    work = [functools.partial(turned, 1)] + [functools.partial(grad, j) for j in range(width // (2 * LANES))]
    interleave(events[-4:], work)
    grads_start()
    rs_end(0)
    events = rs_events(1)
    interleave(events[: len(events) // 2], [functools.partial(give_back, 0, step) for step in range(groups)])
    interleave(events[len(events) // 2 :], [])
    rs_end(1)
    gain_start()
    for step in range(groups):
        give_back(1, step)
    grads_sum()
    gain_turn()
    took = taken(0)
    gain_spread()
    took = took + taken(1)
    center = jnp.zeros((items, 1), F32)
    for q in range(Q):
        cols = slice(q * piece, (q + 1) * piece)
        h = hidden_ref[:, cols].astype(F32)
        center += jnp.sum(igain_ref[:, cols] * took[q * items : (q + 1) * items] * h, axis=-1, keepdims=True)
    center = center / width
    for q in range(Q):
        cols = slice(q * piece, (q + 1) * piece)
        h = hidden_ref[:, cols].astype(F32)
        d = took[q * items : (q + 1) * items]
        dhidden_ref[:, cols] = (
            ifactor * igain_ref[:, cols] * d - h * (ifactor * ifactor * ifactor * center)
        ).astype(BF16)
    for f in range(seqs):
        all_groups(out, arr, f, row_send, row_recv).wait_send()
        all_groups(back_out, back_arr, f, bk_send, bk_recv).wait_send()
        for d in range(2):
            for e in range(hops):
                ag_copy(f, d, e).wait_send()
                rs_copy(f, d, e).wait_send()
        for n in range(1 + 2 * hops):
            sb_copy(f, n).wait_send()
        for k in range(nz):
            mx_copy(f, k).wait_send()
    remote(grad_out.at[gsome], grad_out.at[gsome], gr_send, gr_recv, rep_peer(rep)).wait_send()
    remote(full_ref.at[gsome], full_ref.at[gsome], gg_send, gg_recv, rep_peer(rep)).wait()
    gain_end()


def main(ng, ns, nd, cap, count, owner, row, hidden, igain, ugain, weight, dout):
    items, width = hidden.shape
    seqs, local_len = row.shape
    length = ns * local_len
    owners, msg = ns * nd, cap * Q
    piece = width // Q
    nr, nz = ng * nd, ns // 2
    hops = nz - 1
    cols = 3 * HD
    vmem = pl.BlockSpec(memory_space=pltpu.VMEM)
    full = (width // LANES, cols, LANES)
    dma = pltpu.SemaphoreType.DMA
    return pl.pallas_call(
        functools.partial(main_kernel, ng, ns, nd, cap),
        out_shape=(
            jax.ShapeDtypeStruct((seqs, length, HD), BF16),
            jax.ShapeDtypeStruct((items, width), BF16),
            jax.ShapeDtypeStruct(full, BF16),
            jax.ShapeDtypeStruct((1, width), F32),
            jax.ShapeDtypeStruct((1, width), F32),
        ),
        in_specs=[pl.BlockSpec(memory_space=pltpu.SMEM)] + [vmem] * 5 + [pl.BlockSpec(memory_space=pl.ANY)] * 2,
        out_specs=[vmem] * 5,
        scratch_shapes=[
            pltpu.VMEM((owners, seqs, LANES), jnp.int32),
            pltpu.VMEM((owners, seqs, LANES), jnp.int32),
            pltpu.VMEM((seqs, owners * msg // LANES, 1, LANES), jnp.int32),
            pltpu.VMEM((Q * items, piece), BF16),
            pltpu.VMEM((seqs, owners, msg, piece), BF16),
            pltpu.VMEM((seqs, owners, msg, piece), BF16),
            pltpu.VMEM((seqs, Q * local_len, piece), BF16),
            pltpu.VMEM((seqs, owners, msg, piece), BF16),
            pltpu.VMEM((seqs, owners, msg, piece), BF16),
            pltpu.VMEM((seqs, local_len, width), BF16),
            pltpu.VMEM((seqs, local_len, 1), F32),
            pltpu.VMEM((seqs, local_len, width), BF16),
            pltpu.VMEM((1, width), F32),
            pltpu.VMEM((seqs, ns, local_len, width), BF16),
            pltpu.VMEM((seqs, length, cols), BF16),
            pltpu.VMEM((seqs, length, cols), BF16),
            pltpu.VMEM((cols, seqs * length), BF16),
            pltpu.VMEM((width, cols), BF16),
            pltpu.VMEM((seqs, ns, local_len, width), BF16),
            pltpu.VMEM((seqs, nz, local_len, width), BF16),
            pltpu.VMEM((seqs, 2, hops, local_len // 2, width), BF16),
            pltpu.VMEM((length, HD), F32),
            pltpu.VMEM((length, HD), F32),
            pltpu.VMEM(full, BF16),
            pltpu.VMEM((nr, full[0] // nr, cols, LANES), BF16),
            pltpu.VMEM((2 * Q, 1, piece), F32),
            pltpu.VMEM((ns, 2 * Q // ns, 1, piece), F32),
            pltpu.VMEM((nr, 2 * Q // ns, 1, piece), F32),
            pltpu.VMEM((2 * Q, 1, piece), F32),
            pltpu.VMEM((Q * items, owners * msg), BF16),
            pltpu.VMEM((1, width), F32),
            pltpu.VMEM(weight.shape, BF16),
            pltpu.VMEM(dout.shape, BF16),
            dma((2,)),
        ]
        + [dma] * 2
        + [dma((seqs,))] * 4
        + [dma((seqs, 2, hops))] * 2
        + [dma((seqs, 1 + 2 * hops))] * 2
        + [dma((seqs, nz))] * 2
        + [dma((seqs, 2, hops))] * 2
        + [dma] * 4
        + [dma] * 6,
        compiler_params=pltpu.CompilerParams(
            collective_id=0, has_side_effects=True, vmem_limit_bytes=VMEM_LIMIT
        ),
        name="main",
    )(count, owner, row, hidden, igain, ugain, weight, dout)


def finish_kernel(attn_in, dhidden_in, full_ref, ugrad_in, igrad_in, attn_ref, dhidden_ref, grad_ref, ugrad_ref, igrad_ref):
    @pl.when(pl.program_id(0) == 0)
    def _():
        attn_ref[...] = attn_in[...]
        dhidden_ref[...] = dhidden_in[...]
        ugrad_ref[...] = ugrad_in[...]
        igrad_ref[...] = igrad_in[...]

    for i in range(full_ref.shape[0]):
        grad_ref[0, i * LANES : (i + 1) * LANES, :] = full_ref[i].astype(F32).T


def finish(attn, dhidden, full, ugrad, igrad):
    chunks = full.shape[0]
    width = chunks * LANES

    def whole(a):
        return pl.BlockSpec(a.shape, lambda c: (0,) * len(a.shape))

    return pl.pallas_call(
        finish_kernel,
        grid=(3,),
        out_shape=(
            jax.ShapeDtypeStruct(attn.shape, BF16),
            jax.ShapeDtypeStruct(dhidden.shape, BF16),
            jax.ShapeDtypeStruct((3, width, HD), F32),
            jax.ShapeDtypeStruct(ugrad.shape, F32),
            jax.ShapeDtypeStruct(igrad.shape, F32),
        ),
        in_specs=[whole(attn), whole(dhidden), pl.BlockSpec((chunks, HD, LANES), lambda c: (0, c, 0)), whole(ugrad), whole(igrad)],
        out_specs=[whole(attn), whole(dhidden), pl.BlockSpec((1, width, HD), lambda c: (c, 0, 0)), whole(ugrad), whole(igrad)],
        name="finish",
    )(attn, dhidden, full, ugrad, igrad)


def local(
    item_hidden, item_gain, slot_owner, slot_row, seq_count, user_gain, query_key_value_weight, d_out
):
    ng, ns, nd = (lax.axis_size(a) for a in ("grp", "seq", "dp"))
    seqs, local_len, _ = slot_owner.shape
    width = item_hidden.shape[1]
    cap = max(2, 2 * local_len // (ns * nd))
    igain, ugain = item_gain.reshape(1, width), user_gain.reshape(1, width)
    owner = slot_owner.transpose(0, 2, 1)
    attn, d_hidden, full, ugrad, igrad = main(
        ng, ns, nd, cap, seq_count, owner, slot_row, item_hidden, igain, ugain, query_key_value_weight, d_out
    )
    attn, d_hidden, grads, ugrad, igrad = finish(attn, d_hidden, full, ugrad, igrad)
    return (attn, d_hidden, grads, ugrad.reshape(width), igrad.reshape(width))


def solution(mesh):
    in_specs = (
        P(("grp", "seq", "dp"), None),
        P(),
        P(("grp", "dp"), "seq", None),
        P(("grp", "dp"), "seq"),
        P(("grp", "dp")),
        P(),
        P(None, None, "seq"),
        P(("grp", "dp"), None, "seq"),
    )
    out_specs = (
        P(("grp", "dp"), None, "seq"),
        P(("grp", "seq", "dp"), None),
        P(None, None, "seq"),
        P(),
        P(),
    )
    return jax.shard_map(local, mesh=mesh, in_specs=in_specs, out_specs=out_specs, check_vma=False)
```

```python
import functools
import math

import jax
import jax.numpy as jnp
from jax import lax
from jax.experimental import pallas as pl
from jax.experimental.pallas import tpu as pltpu
from jax.sharding import PartitionSpec as P

HD = 128
LANES = 128
Q = 8
EPS = 1e-05
MESH = pl.DeviceIdType.MESH
F32, BF16 = jnp.float32, jnp.bfloat16
VMEM_LIMIT = 60 * 2**20


def iota(shape, dim):
    return lax.broadcasted_iota(jnp.int32, shape, dim).astype(F32)


def onehot(mask):
    return jnp.where(mask, 1.0, 0.0).astype(BF16)


def column(row):
    return jnp.broadcast_to(row, (LANES, LANES)).T


def plane_peer(index, nd):
    return {"seq": index // nd, "dp": lax.rem(index, nd)}


def greet(barrier, device):
    pl.semaphore_signal(barrier, inc=1, device_id=device, device_id_type=MESH)


def remote(src, dst, send, recv, device):
    return pltpu.make_async_remote_copy(
        src_ref=src, dst_ref=dst, send_sem=send, recv_sem=recv, device_id=device, device_id_type=MESH
    )


def slots(owner_ref, cap, f):
    own = owner_ref[f].astype(F32)
    length = own.shape[1]
    owner_row = jnp.concatenate([own, own], axis=1)
    owner = jnp.broadcast_to(owner_row, (LANES, LANES))
    this = iota((LANES, LANES), 1)
    this = jnp.where(this >= length, this - length, this)
    earlier = (owner == owner.T) & (iota((LANES, LANES), 0) < this)
    rank_row = jnp.sum(jnp.where(earlier, 1.0, 0.0), axis=0, keepdims=True)
    return owner_row, rank_row, (owner_row * cap + rank_row) * Q


def main_kernel(
    ng, ns, nd, cap,
    count_ref, owner_ref, row_ref, hidden_ref, igain_ref, ugain_ref, weight_in, dout_in,
    attn_ref, dhidden_ref, full_ref, ugrad_ref, igrad_ref,
    req, reqr, val, table, out, arr, stack, back_out, back_arr,
    inputs, ufactor, dinputs, uterms,
    gat, prj, dpr, dpt, wgt, part, mix, ring, dk_acc, dv_acc,
    grad_out, gin, tmine, tin, tmid, tall, picks, iterms, weight_ref, dout_ref, load_sem,
    id_send, id_recv, row_send, row_recv, bk_send, bk_recv,
    ag_send, ag_recv, sb_send, sb_recv, mx_send, mx_recv, rs_send, rs_recv,
    gr_send, gr_recv, gg_send, gg_recv, t_send, t_recv, u_send, u_recv, v_send, v_recv,
):
    seqs, _, local_len, width = gat.shape
    items = hidden_ref.shape[0]
    length = ns * local_len
    owners, msg = ns * nd, cap * Q
    per_g = LANES // msg
    groups = owners // per_g
    piece = width // Q
    nr = ng * nd
    nz = ns // 2
    half = nz // 2
    hops = 2 * half - 1
    hl = local_len // 2
    per = 4
    tile = per * local_len
    tiles = ns // per
    seq, dp, grp = lax.axis_index("seq"), lax.axis_index("dp"), lax.axis_index("grp")
    me = seq * nd + dp
    rep = grp * nd + dp
    z, core = seq // 2, lax.rem(seq, 2)
    sib_index = seq + 1 - 2 * core
    sib = {"seq": sib_index}
    ahead = ({"seq": lax.rem(seq + 2, ns)}, {"seq": lax.rem(seq + ns - 2, ns)})
    scale = 1.0 / math.sqrt(HD)
    my_group = me // per_g

    def rep_peer(index):
        return {"grp": index // nd, "dp": lax.rem(index, nd)}

    def turn_of(step):
        far = groups // 2 - (step + 1) // 2
        return lax.rem(my_group + (far if step % 2 == 0 else groups - far), groups)

    barrier = pltpu.get_barrier_semaphore()
    loads = (
        pltpu.make_async_copy(weight_in, weight_ref, load_sem.at[0]),
        pltpu.make_async_copy(dout_in, dout_ref, load_sem.at[1]),
    )
    for load in loads:
        load.start()

    @pl.loop(1, owners)
    def _(i):
        greet(barrier, plane_peer(lax.rem(me + i, owners), nd))

    @pl.loop(nd, nr)
    def _(i):
        greet(barrier, rep_peer(lax.rem(grp * nd + i, nr)))

    lane = lax.broadcasted_iota(jnp.int32, (LANES, LANES), 1)
    slot_in = ((lane % msg) // Q).astype(F32)
    piece_of = (lane[0:1, :] % Q).astype(F32)
    places = []
    for f in range(seqs):
        owner_row, rank_row, base_row = slots(owner_ref, cap, f)
        places.append(base_row)
        want = row_ref[f : f + 1, :].astype(F32) + 1.0
        row_col = column(jnp.concatenate([want, jnp.zeros_like(want)], axis=1))
        wanted = jnp.where(column(rank_row) == slot_in, row_col, 0.0).astype(BF16)
        names = onehot(iota((owners, LANES), 0) == owner_row)
        asked = jnp.dot(names, wanted, preferred_element_type=F32)
        asked = jnp.where(asked > 0.5, asked - 1.0 + piece_of * items, -1.0).astype(jnp.int32)
        for o in range(owners):
            req[o, f : f + 1, :] = asked[o : o + 1, :]

    pl.semaphore_wait(barrier, owners - 1 + nr - nd)

    @pl.loop(1, owners)
    def _(i):
        peer = lax.rem(me + i, owners)
        remote(req.at[peer], reqr.at[me], id_send, id_recv, plane_peer(peer, nd)).start()

    reqr[me] = req[me]
    hidden = hidden_ref[...].astype(F32)
    ifactor = lax.rsqrt(jnp.mean(hidden * hidden, axis=-1, keepdims=True) + EPS)
    for q in range(Q):
        cols = slice(q * piece, (q + 1) * piece)
        table[q * items : (q + 1) * items, :] = (
            hidden_ref[:, cols].astype(F32) * ifactor * igain_ref[:, cols]
        ).astype(BF16)
    remote(
        req.at[pl.ds(0, owners - 1)], reqr.at[pl.ds(0, owners - 1)], id_send, id_recv, plane_peer(me, nd)
    ).wait()

    def send_group(src, dst, f, g, send, recv):
        for k in range(per_g):
            peer = g * per_g + k

            @pl.when(peer != me)
            def _():
                remote(src.at[f, peer], dst.at[f, me], send.at[f], recv.at[f], plane_peer(peer, nd)).start()

    def all_groups(src, dst, f, send, recv):
        some = pl.ds(0, owners - 1)
        return remote(src.at[f, some], dst.at[f, some], send.at[f], recv.at[f], plane_peer(me, nd))

    lane_group = lax.broadcasted_iota(jnp.int32, (1, LANES), 1) // msg

    def fetch(f, step):
        g = turn_of(step)
        ids = jnp.zeros((1, LANES), jnp.int32)
        for k in range(per_g):
            ids = jnp.where(lane_group == k, reqr[g * per_g + k][f : f + 1, :], ids)
        val[f, g] = ids
        col = column(ids.astype(F32))
        pick = jnp.concatenate([onehot(col == iota((LANES, LANES), 1) + q * items) for q in range(Q)], axis=1)
        picked = jnp.dot(pick, table[...], preferred_element_type=F32).astype(BF16)
        out[f, pl.ds(g * per_g, per_g)] = picked.reshape(per_g, msg, piece)
        send_group(out, arr, f, g, row_send, row_recv)

    def place(f):
        arr[f, me] = out[f, me]
        base_col = column(places[f])[0:local_len]
        all_groups(out, arr, f, row_send, row_recv).wait_recv()
        arrived = arr[f].reshape(owners * msg, piece)
        total = jnp.zeros((local_len, 1), F32)
        wanted_at = jnp.concatenate([base_col + q for q in range(Q)], axis=0)
        put = jnp.concatenate(
            [onehot(iota(wanted_at.shape, 1) + t * LANES == wanted_at) for t in range(groups)], axis=1
        )
        placed = jnp.dot(put, arrived, preferred_element_type=F32)
        for q in range(Q):
            rows = placed[q * local_len : (q + 1) * local_len]
            inputs[f, :, q * piece : (q + 1) * piece] = rows.astype(BF16)
            total += jnp.sum(rows * rows, axis=-1, keepdims=True)
        factor = lax.rsqrt(total / width + EPS)
        ufactor[f] = factor
        gat[f, seq] = (inputs[f].astype(F32) * factor * ugain_ref[...]).astype(BF16)

    def give_back(f, step):
        if step == 0:
            for q in range(Q):
                stack[f, q * local_len : (q + 1) * local_len, :] = dinputs[f, :, q * piece : (q + 1) * piece]
        g = turn_of(step)
        rows = iota((LANES, LANES), 0) + (g * LANES).astype(F32)
        second = jnp.where(iota((1, LANES), 1) >= local_len, 1.0, 0.0)
        put = jnp.concatenate([onehot(rows == places[f] + (2.0 * t + second)) for t in range(Q // 2)], axis=1)
        sent = jnp.dot(put, stack[f], preferred_element_type=F32).astype(BF16)
        back_out[f, pl.ds(g * per_g, per_g)] = sent.reshape(per_g, msg, piece)
        send_group(back_out, back_arr, f, g, bk_send, bk_recv)

    def taken(f):
        back_arr[f, me] = back_out[f, me]
        for g in range(groups):
            picks[:, g * LANES : (g + 1) * LANES] = onehot(iota((Q * items, LANES), 0) == val[f, g].astype(F32))
        all_groups(back_out, back_arr, f, bk_send, bk_recv).wait_recv()
        return jnp.dot(picks[...], back_arr[f].reshape(owners * msg, piece), preferred_element_type=F32)

    def ag_place(f, d, e, origin):
        far = e // 2
        h = d if e == hops - 1 else e % 2
        block = lax.rem(origin + (ns - 2 * far if d == 0 else 2 * far), ns)
        return gat.at[f, block, pl.ds(h * hl, hl)]

    def ag_copy(f, d, e):
        ref = ag_place(f, d, e, seq)
        return remote(ref, ref, ag_send.at[f, d, e], ag_recv.at[f, d, e], ahead[d])

    def ag_arrival(f, d, e, at):
        behind = lax.rem(at + (ns - 2 if d == 0 else 2), ns)
        return ag_place(f, d, e, behind)

    def ag_wait(f, d, e):
        ref = ag_arrival(f, d, e, seq)
        remote(ref, ref, ag_send.at[f, d, e], ag_recv.at[f, d, e], ahead[d]).wait_recv()

    def sb_copy(f, n):
        ref = gat.at[f, seq] if n == 0 else ag_arrival(f, (n - 1) % 2, (n - 1) // 2, seq)
        return remote(ref, ref, sb_send.at[f, n], sb_recv.at[f, n], sib)

    def sb_wait(f, n):
        ref = gat.at[f, sib_index] if n == 0 else ag_arrival(f, (n - 1) % 2, (n - 1) // 2, sib_index)
        remote(ref, ref, sb_send.at[f, n], sb_recv.at[f, n], sib).wait_recv()

    def ag_begin(f):
        for e in range(min(2, hops)):
            for d in range(2):
                ag_copy(f, d, e).start()
        sb_copy(f, 0).start()

    def ag_event(f, d, e):
        ag_wait(f, d, e)
        if e + 2 < hops - 1:
            ag_copy(f, d, e + 2).start()
        elif e + 2 == hops - 1 + d:
            ag_copy(f, d, hops - 1).start()
        sb_copy(f, 1 + 2 * e + d).start()

    def ag_events(f):
        return [functools.partial(ag_event, f, d, e) for e in range(hops) for d in range(2)]

    def ag_end(f):
        for n in range(1 + 2 * hops):
            sb_wait(f, n)

    order = [(half, None)] + [(t, h) for t in range(half - 1, 0, -1) for h in range(2)]

    def rs_what(d, i):
        t, h = order[i]
        return t, d if h is None else h

    def chip(d, t):
        return lax.rem(z + (t if d == 0 else nz - t), nz)

    def rs_copy(f, d, i):
        t, h = rs_what(d, i)
        return remote(
            mix.at[f, chip(d, t), pl.ds(h * hl, hl)], ring.at[f, d, i], rs_send.at[f, d, i], rs_recv.at[f, d, i], ahead[d]
        )

    def mx_copy(f, k):
        return remote(part.at[f, 2 * k + 1 - core], mix.at[f, k], mx_send.at[f, k], mx_recv.at[f, k], sib)

    def own_sum(f, k):
        mix[f, k] = (mix[f, k].astype(F32) + part[f, 2 * k + core].astype(F32)).astype(BF16)

    def rs_source(d, i):
        t, h = rs_what(d, i)
        for j in range(len(order)):
            if rs_what(d, j) == (t + 1, h):
                return j
        return None

    def rs_own(f, t):
        own_sum(f, chip(0, t))
        if 0 < t < half:
            own_sum(f, chip(1, t))
        for d in range(2):
            for i in range(len(order)):
                if rs_what(d, i)[0] == t and rs_source(d, i) is None:
                    rs_copy(f, d, i).start()

    def rs_start(f):
        for k in range(nz):
            mx_copy(f, k).wait_recv()
        rs_own(f, half)
        rs_own(f, half - 1)

    def rs_event(f, d, j):
        rs_copy(f, d, j).wait_recv()
        t, h = rs_what(d, j)
        if t == 1:
            return
        for i in range(len(order)):
            if rs_what(d, i) == (t - 1, h):
                rows = pl.ds(h * hl, hl)
                k = chip(d, t - 1)
                mix[f, k, rows] = (mix[f, k, rows].astype(F32) + ring[f, d, j].astype(F32)).astype(BF16)
                rs_copy(f, d, i).start()

    def rs_events(f):
        events = [functools.partial(rs_own, f, t) for t in range(half - 2, -1, -1)]
        return events + [functools.partial(rs_event, f, d, j) for j in range(len(order)) for d in range(2)]

    def rs_end(f):
        total = mix[f, z].astype(F32)
        for h in range(2):
            rows = slice(h * hl, (h + 1) * hl)
            got = total[rows]
            for d in range(2):
                for i in range(len(order)):
                    if rs_what(d, i) == (1, h):
                        got = got + ring[f, d, i].astype(F32)
            values = inputs[f, rows, :].astype(F32)
            factor = ufactor[f, rows, :]
            weighted = ugain_ref[...] * got
            center = jnp.mean(weighted * values, axis=-1, keepdims=True)
            d_in = factor * weighted - values * (factor * factor * factor * center)
            dinputs[f, rows, :] = d_in.astype(BF16)
            for ref, term in ((uterms, got * values * factor), (iterms, d_in * values)):
                term = jnp.sum(term, axis=0, keepdims=True)
                if f == 0 and h == 0:
                    ref[...] = term
                else:
                    ref[...] += term

    def project(f, i):
        rows = gat[f, i * per : (i + 1) * per].reshape(tile, width)
        prj[f, i * tile : (i + 1) * tile, :] = jnp.dot(rows, wgt[...], preferred_element_type=F32).astype(BF16)

    def attend(f, i):
        keys_n = (i + 1) * tile
        at = slice(i * tile, (i + 1) * tile)
        query = prj[f, at, 0:HD]
        keys = prj[f, 0:keys_n, HD : 2 * HD]
        values = prj[f, 0:keys_n, 2 * HD : 3 * HD]
        upstream = dout_ref[f, at, :]
        over = (((1,), (1,)), ((), ()))
        down = (((0,), (0,)), ((), ()))
        scores = lax.dot_general(query, keys, over, preferred_element_type=F32) * scale
        p = lax.broadcasted_iota(jnp.int32, (tile, keys_n), 0) + i * tile
        k = lax.broadcasted_iota(jnp.int32, (tile, keys_n), 1)
        allowed = (k <= p) & (k < count_ref[f])
        scores = jnp.where(allowed, scores, -1e30)
        exponent = jnp.exp(scores - jnp.max(scores, axis=-1, keepdims=True))
        weights = exponent * (1.0 / jnp.sum(exponent, axis=-1, keepdims=True))
        weights_b = weights.astype(BF16)
        attn_ref[f, at, :] = jnp.dot(weights_b, values, preferred_element_type=F32).astype(BF16)
        d_weights = lax.dot_general(upstream, values, over, preferred_element_type=F32)
        center = jnp.sum(weights * d_weights, axis=-1, keepdims=True)
        d_scores = (weights * (d_weights - center) * scale).astype(BF16)
        dpr[f, at, 0:HD] = jnp.dot(d_scores, keys, preferred_element_type=F32).astype(BF16)
        d_values = lax.dot_general(weights_b, upstream, down, preferred_element_type=F32)
        d_keys = lax.dot_general(d_scores, query, down, preferred_element_type=F32)
        old = i * tile
        if i:
            dv_acc[0:old, :] += d_values[0:old]
            dk_acc[0:old, :] += d_keys[0:old]
        dv_acc[at, :] = d_values[old:]
        dk_acc[at, :] = d_keys[old:]

    def attended(f):
        dpr[f, :, HD : 2 * HD] = dk_acc[...].astype(BF16)
        dpr[f, :, 2 * HD : 3 * HD] = dv_acc[...].astype(BF16)

    def back(f, i):
        rows = dpr[f, i * tile : (i + 1) * tile, :]
        term = lax.dot_general(rows, wgt[...], (((1,), (1,)), ((), ())), preferred_element_type=F32)
        part[f, i * per : (i + 1) * per] = term.astype(BF16).reshape(per, local_len, width)
        for k in range(per // 2):
            mx_copy(f, i * per // 2 + k).start()

    def turned(f):
        dpt[:, f * length : (f + 1) * length] = dpr[f].T

    def grad(j):
        cols = slice(j * 2 * LANES, (j + 1) * 2 * LANES)
        got = jnp.zeros((dpt.shape[0], 2 * LANES), F32)
        for f in range(seqs):
            rows = gat[f, :, :, cols].reshape(length, 2 * LANES)
            got += jnp.dot(dpt[:, f * length : (f + 1) * length], rows, preferred_element_type=F32)
        for k in range(2):
            grad_out[2 * j + k] = got[:, k * LANES : (k + 1) * LANES].astype(BF16)

    gchunk = width // LANES // nr
    gmine = pl.ds(rep * gchunk, gchunk)
    gsome = pl.ds(0, (nr - 1) * gchunk)

    away = sorted(
        ((a, b) for a in range(ng) for b in range(nd) if a or b),
        key=lambda o: (min(o[0], ng - o[0]) + min(o[1], nd - o[1]), (o[0] + 2 * o[1]) % 3, o),
    )

    def rep_at(a, b):
        return lax.rem(grp + a, ng) * nd + lax.rem(dp + b, nd)

    def grads_start():
        for a, b in away:
            peer = rep_at(a, b)
            remote(grad_out.at[pl.ds(peer * gchunk, gchunk)], gin.at[rep], gr_send, gr_recv, rep_peer(peer)).start()

        gin[rep] = grad_out[gmine]

    def grads_sum():
        remote(grad_out.at[gsome], grad_out.at[gsome], gr_send, gr_recv, rep_peer(rep)).wait_recv()
        got = gin[0].astype(F32)
        for i in range(1, nr):
            got += gin[i].astype(F32)
        full_ref[gmine] = got.astype(BF16)

        for a in range(1, ng):
            gg_own(0, {"grp": lax.rem(grp + a, ng)}).start()
        for b in range(1, nd):
            gg_own(1, {"dp": lax.rem(dp + b, nd)}).start()

    def gg_own(way, device):
        return remote(full_ref.at[gmine], full_ref.at[gmine], gg_send.at[way], gg_recv.at[way], device)

    def gg_first(way):
        some = full_ref.at[pl.ds(0, (ng if way == 0 else nd) * gchunk - gchunk)]
        return remote(some, some, gg_send.at[way], gg_recv.at[way], rep_peer(rep))

    def gg_half(way):
        size = full_ref.shape[1] // 2
        return pl.ds(way * size, size)

    def gg_rest(way):
        some = full_ref.at[pl.ds(0, (ng - 1) * (nd - 1) * gchunk), gg_half(way)]
        return remote(some, some, gg_send.at[2 + way], gg_recv.at[2 + way], rep_peer(rep))

    def grads_spread():
        if ng > 1:
            gg_first(0).wait_recv()
        for a in range(1, ng):
            there = full_ref.at[pl.ds(rep_at(a, 0) * gchunk, gchunk), gg_half(0)]
            for b in range(1, nd):
                remote(there, there, gg_send.at[2], gg_recv.at[2], {"dp": lax.rem(dp + b, nd)}).start()
        if nd > 1:
            gg_first(1).wait_recv()
        for b in range(1, nd):
            there = full_ref.at[pl.ds(rep_at(0, b) * gchunk, gchunk), gg_half(1)]
            for a in range(1, ng):
                remote(there, there, gg_send.at[3], gg_recv.at[3], {"grp": lax.rem(grp + a, ng)}).start()

    def grads_end():
        for way in range(2):
            if (ng, nd)[way] > 1:
                gg_first(way).wait_send()
            if ng > 1 and nd > 1:
                gg_rest(way).wait()

    rp = 2 * Q // ns
    tsome = pl.ds(0, ns - 1)

    def gain_start():
        for q in range(Q):
            cols = slice(q * piece, (q + 1) * piece)
            tmine[q] = iterms[:, cols] / igain_ref[:, cols]
            tmine[Q + q] = uterms[:, cols]

        @pl.loop(1, ns)
        def _(i):
            peer = lax.rem(seq + i, ns)
            remote(tmine.at[pl.ds(peer * rp, rp)], tin.at[seq], t_send, t_recv, {"seq": peer}).start()

        tin[seq] = tmine[pl.ds(seq * rp, rp)]

    def gain_turn():
        remote(tin.at[tsome], tin.at[tsome], t_send, t_recv, {"seq": seq}).wait()
        total = tin[0]
        for i in range(1, ns):
            total = total + tin[i]
        tmid[rep] = total
        for a, b in away:
            remote(tmid.at[rep], tmid.at[rep], u_send, u_recv, rep_peer(rep_at(a, b))).start()

    def gain_spread():
        some = pl.ds(0, nr - 1)
        remote(tmid.at[some], tmid.at[some], u_send, u_recv, rep_peer(rep)).wait()
        total = tmid[0]
        for i in range(1, nr):
            total = total + tmid[i]
        mine = pl.ds(seq * rp, rp)
        tall[mine] = total

        @pl.loop(1, ns)
        def _(i):
            remote(tall.at[mine], tall.at[mine], v_send, v_recv, {"seq": lax.rem(seq + i, ns)}).start()

    def gain_end():
        some = pl.ds(0, (ns - 1) * rp)
        remote(tall.at[some], tall.at[some], v_send, v_recv, {"seq": seq}).wait()
        for q in range(Q):
            cols = slice(q * piece, (q + 1) * piece)
            igrad_ref[:, cols] = tall[q]
            ugrad_ref[:, cols] = tall[Q + q]

    def sequence_work(f):
        work = [functools.partial(project, f, i) for i in range(tiles)]
        work += [functools.partial(attend, f, i) for i in range(tiles)]
        work += [functools.partial(attended, f)]
        return work + [functools.partial(back, f, i) for i in range(tiles)]

    def interleave(events, work):
        done = 0
        for n, event in enumerate(events):
            event()
            upto = (n + 1) * len(work) // len(events)
            for item in work[done:upto]:
                item()
            done = upto
        for item in work[done:]:
            item()

    for f in range(seqs):
        for step in range(groups):
            fetch(f, step)
    for load in loads:
        load.wait()
    for c in range(3):
        wgt[:, c * HD : (c + 1) * HD] = weight_ref[c]
    place(0)
    ag_begin(0)
    events = ag_events(0)
    first, last = 2 * hops // 4, 2 * hops // 2
    interleave(events[:first], [])
    place(1)
    interleave(events[first:last], [])
    ag_begin(1)
    interleave(events[last:], [])
    ag_end(0)
    events = ag_events(1)
    interleave(events[:-4], sequence_work(0))
    rs_start(0)
    interleave(events[-4:], [])
    ag_end(1)
    events = rs_events(0)
    interleave(events[:-4], [functools.partial(turned, 0)] + sequence_work(1))
    rs_start(1)
    work = [functools.partial(turned, 1)] + [functools.partial(grad, j) for j in range(width // (2 * LANES))]
    interleave(events[-4:], work)
    grads_start()
    rs_end(0)
    events = rs_events(1)
    interleave(events[: len(events) // 2], [functools.partial(give_back, 0, step) for step in range(groups)])
    interleave(events[len(events) // 2 : -2], [])
    grads_sum()
    interleave(events[-2:], [])
    rs_end(1)
    gain_start()
    for step in range(groups):
        give_back(1, step)
    grads_spread()
    gain_turn()
    took = taken(0)
    gain_spread()
    took = took + taken(1)
    center = jnp.zeros((items, 1), F32)
    for q in range(Q):
        cols = slice(q * piece, (q + 1) * piece)
        h = hidden_ref[:, cols].astype(F32)
        center += jnp.sum(igain_ref[:, cols] * took[q * items : (q + 1) * items] * h, axis=-1, keepdims=True)
    center = center / width
    for q in range(Q):
        cols = slice(q * piece, (q + 1) * piece)
        h = hidden_ref[:, cols].astype(F32)
        d = took[q * items : (q + 1) * items]
        dhidden_ref[:, cols] = (
            ifactor * igain_ref[:, cols] * d - h * (ifactor * ifactor * ifactor * center)
        ).astype(BF16)
    for f in range(seqs):
        all_groups(out, arr, f, row_send, row_recv).wait_send()
        all_groups(back_out, back_arr, f, bk_send, bk_recv).wait_send()
        for d in range(2):
            for e in range(hops):
                ag_copy(f, d, e).wait_send()
                rs_copy(f, d, e).wait_send()
        for n in range(1 + 2 * hops):
            sb_copy(f, n).wait_send()
        for k in range(nz):
            mx_copy(f, k).wait_send()
    remote(grad_out.at[gsome], grad_out.at[gsome], gr_send, gr_recv, rep_peer(rep)).wait_send()
    grads_end()
    gain_end()


def main(ng, ns, nd, cap, count, owner, row, hidden, igain, ugain, weight, dout):
    items, width = hidden.shape
    seqs, local_len = row.shape
    length = ns * local_len
    owners, msg = ns * nd, cap * Q
    piece = width // Q
    nr, nz = ng * nd, ns // 2
    hops = nz - 1
    cols = 3 * HD
    vmem = pl.BlockSpec(memory_space=pltpu.VMEM)
    full = (width // LANES, cols, LANES)
    dma = pltpu.SemaphoreType.DMA
    return pl.pallas_call(
        functools.partial(main_kernel, ng, ns, nd, cap),
        out_shape=(
            jax.ShapeDtypeStruct((seqs, length, HD), BF16),
            jax.ShapeDtypeStruct((items, width), BF16),
            jax.ShapeDtypeStruct(full, BF16),
            jax.ShapeDtypeStruct((1, width), F32),
            jax.ShapeDtypeStruct((1, width), F32),
        ),
        in_specs=[pl.BlockSpec(memory_space=pltpu.SMEM)] + [vmem] * 5 + [pl.BlockSpec(memory_space=pl.ANY)] * 2,
        out_specs=[vmem] * 5,
        scratch_shapes=[
            pltpu.VMEM((owners, seqs, LANES), jnp.int32),
            pltpu.VMEM((owners, seqs, LANES), jnp.int32),
            pltpu.VMEM((seqs, owners * msg // LANES, 1, LANES), jnp.int32),
            pltpu.VMEM((Q * items, piece), BF16),
            pltpu.VMEM((seqs, owners, msg, piece), BF16),
            pltpu.VMEM((seqs, owners, msg, piece), BF16),
            pltpu.VMEM((seqs, Q * local_len, piece), BF16),
            pltpu.VMEM((seqs, owners, msg, piece), BF16),
            pltpu.VMEM((seqs, owners, msg, piece), BF16),
            pltpu.VMEM((seqs, local_len, width), BF16),
            pltpu.VMEM((seqs, local_len, 1), F32),
            pltpu.VMEM((seqs, local_len, width), BF16),
            pltpu.VMEM((1, width), F32),
            pltpu.VMEM((seqs, ns, local_len, width), BF16),
            pltpu.VMEM((seqs, length, cols), BF16),
            pltpu.VMEM((seqs, length, cols), BF16),
            pltpu.VMEM((cols, seqs * length), BF16),
            pltpu.VMEM((width, cols), BF16),
            pltpu.VMEM((seqs, ns, local_len, width), BF16),
            pltpu.VMEM((seqs, nz, local_len, width), BF16),
            pltpu.VMEM((seqs, 2, hops, local_len // 2, width), BF16),
            pltpu.VMEM((length, HD), F32),
            pltpu.VMEM((length, HD), F32),
            pltpu.VMEM(full, BF16),
            pltpu.VMEM((nr, full[0] // nr, cols, LANES), BF16),
            pltpu.VMEM((2 * Q, 1, piece), F32),
            pltpu.VMEM((ns, 2 * Q // ns, 1, piece), F32),
            pltpu.VMEM((nr, 2 * Q // ns, 1, piece), F32),
            pltpu.VMEM((2 * Q, 1, piece), F32),
            pltpu.VMEM((Q * items, owners * msg), BF16),
            pltpu.VMEM((1, width), F32),
            pltpu.VMEM(weight.shape, BF16),
            pltpu.VMEM(dout.shape, BF16),
            dma((2,)),
        ]
        + [dma] * 2
        + [dma((seqs,))] * 4
        + [dma((seqs, 2, hops))] * 2
        + [dma((seqs, 1 + 2 * hops))] * 2
        + [dma((seqs, nz))] * 2
        + [dma((seqs, 2, hops))] * 2
        + [dma] * 2
        + [dma((4,))] * 2
        + [dma] * 6,
        compiler_params=pltpu.CompilerParams(
            collective_id=0, has_side_effects=True, vmem_limit_bytes=VMEM_LIMIT
        ),
        name="main",
    )(count, owner, row, hidden, igain, ugain, weight, dout)


def finish_kernel(attn_in, dhidden_in, full_ref, ugrad_in, igrad_in, attn_ref, dhidden_ref, grad_ref, ugrad_ref, igrad_ref):
    @pl.when(pl.program_id(0) == 0)
    def _():
        attn_ref[...] = attn_in[...]
        dhidden_ref[...] = dhidden_in[...]
        ugrad_ref[...] = ugrad_in[...]
        igrad_ref[...] = igrad_in[...]

    for i in range(full_ref.shape[0]):
        grad_ref[0, i * LANES : (i + 1) * LANES, :] = full_ref[i].astype(F32).T


def finish(attn, dhidden, full, ugrad, igrad):
    chunks = full.shape[0]
    width = chunks * LANES

    def whole(a):
        return pl.BlockSpec(a.shape, lambda c: (0,) * len(a.shape))

    return pl.pallas_call(
        finish_kernel,
        grid=(3,),
        out_shape=(
            jax.ShapeDtypeStruct(attn.shape, BF16),
            jax.ShapeDtypeStruct(dhidden.shape, BF16),
            jax.ShapeDtypeStruct((3, width, HD), F32),
            jax.ShapeDtypeStruct(ugrad.shape, F32),
            jax.ShapeDtypeStruct(igrad.shape, F32),
        ),
        in_specs=[whole(attn), whole(dhidden), pl.BlockSpec((chunks, HD, LANES), lambda c: (0, c, 0)), whole(ugrad), whole(igrad)],
        out_specs=[whole(attn), whole(dhidden), pl.BlockSpec((1, width, HD), lambda c: (c, 0, 0)), whole(ugrad), whole(igrad)],
        name="finish",
    )(attn, dhidden, full, ugrad, igrad)


def local(
    item_hidden, item_gain, slot_owner, slot_row, seq_count, user_gain, query_key_value_weight, d_out
):
    ng, ns, nd = (lax.axis_size(a) for a in ("grp", "seq", "dp"))
    seqs, local_len, _ = slot_owner.shape
    width = item_hidden.shape[1]
    cap = max(2, 2 * local_len // (ns * nd))
    igain, ugain = item_gain.reshape(1, width), user_gain.reshape(1, width)
    owner = slot_owner.transpose(0, 2, 1)
    attn, d_hidden, full, ugrad, igrad = main(
        ng, ns, nd, cap, seq_count, owner, slot_row, item_hidden, igain, ugain, query_key_value_weight, d_out
    )
    attn, d_hidden, grads, ugrad, igrad = finish(attn, d_hidden, full, ugrad, igrad)
    return (attn, d_hidden, grads, ugrad.reshape(width), igrad.reshape(width))


def solution(mesh):
    in_specs = (
        P(("grp", "seq", "dp"), None),
        P(),
        P(("grp", "dp"), "seq", None),
        P(("grp", "dp"), "seq"),
        P(("grp", "dp")),
        P(),
        P(None, None, "seq"),
        P(("grp", "dp"), None, "seq"),
    )
    out_specs = (
        P(("grp", "dp"), None, "seq"),
        P(("grp", "seq", "dp"), None),
        P(None, None, "seq"),
        P(),
        P(),
    )
    return jax.shard_map(local, mesh=mesh, in_specs=in_specs, out_specs=out_specs, check_vma=False)
```

```python
import functools
import math

import jax
import jax.numpy as jnp
from jax import lax
from jax.experimental import pallas as pl
from jax.experimental.pallas import tpu as pltpu
from jax.sharding import PartitionSpec as P

HD = 128
LANES = 128
Q = 8
EPS = 1e-05
MESH = pl.DeviceIdType.MESH
F32, BF16 = jnp.float32, jnp.bfloat16
VMEM_LIMIT = 60 * 2**20


def iota(shape, dim):
    return lax.broadcasted_iota(jnp.int32, shape, dim).astype(F32)


def onehot(mask):
    return jnp.where(mask, 1.0, 0.0).astype(BF16)


def column(row):
    return jnp.broadcast_to(row, (LANES, LANES)).T


def plane_peer(index, nd):
    return {"seq": index // nd, "dp": lax.rem(index, nd)}


def greet(barrier, device):
    pl.semaphore_signal(barrier, inc=1, device_id=device, device_id_type=MESH)


def remote(src, dst, send, recv, device):
    return pltpu.make_async_remote_copy(
        src_ref=src, dst_ref=dst, send_sem=send, recv_sem=recv, device_id=device, device_id_type=MESH
    )


def slots(owner_ref, cap, f):
    own = owner_ref[f].astype(F32)
    length = own.shape[1]
    owner_row = jnp.concatenate([own, own], axis=1)
    owner = jnp.broadcast_to(owner_row, (LANES, LANES))
    this = iota((LANES, LANES), 1)
    this = jnp.where(this >= length, this - length, this)
    earlier = (owner == owner.T) & (iota((LANES, LANES), 0) < this)
    rank_row = jnp.sum(jnp.where(earlier, 1.0, 0.0), axis=0, keepdims=True)
    return owner_row, rank_row, (owner_row * cap + rank_row) * Q


def main_kernel(
    ng, ns, nd, cap,
    count_ref, owner_ref, row_ref, hidden_ref, igain_ref, ugain_ref, weight_in, dout_in,
    attn_ref, dhidden_ref, full_ref, ugrad_ref, igrad_ref,
    req, reqr, val, table, out, arr, stack, back_out, back_arr,
    inputs, ufactor, dinputs, uterms,
    gat, prj, dpr, dpt, wgt, part, mix, ring, dk_acc, dv_acc,
    grad_out, gin, tmine, tin, tmid, tall, picks, iterms, weight_ref, dout_ref, load_sem,
    id_send, id_recv, row_send, row_recv, bk_send, bk_recv,
    ag_send, ag_recv, sb_send, sb_recv, mx_send, mx_recv, rs_send, rs_recv,
    gr_send, gr_recv, gg_send, gg_recv, t_send, t_recv, u_send, u_recv, v_send, v_recv,
):
    seqs, _, local_len, width = gat.shape
    items = hidden_ref.shape[0]
    length = ns * local_len
    owners, msg = ns * nd, cap * Q
    per_g = LANES // msg
    groups = owners // per_g
    piece = width // Q
    nr = ng * nd
    nz = ns // 2
    half = nz // 2
    hops = 2 * half - 1
    hl = local_len // 2
    per = 4
    tile = per * local_len
    tiles = ns // per
    seq, dp, grp = lax.axis_index("seq"), lax.axis_index("dp"), lax.axis_index("grp")
    me = seq * nd + dp
    rep = grp * nd + dp
    z, core = seq // 2, lax.rem(seq, 2)
    sib_index = seq + 1 - 2 * core
    sib = {"seq": sib_index}
    ahead = ({"seq": lax.rem(seq + 2, ns)}, {"seq": lax.rem(seq + ns - 2, ns)})
    scale = 1.0 / math.sqrt(HD)
    my_group = me // per_g

    def rep_peer(index):
        return {"grp": index // nd, "dp": lax.rem(index, nd)}

    def turn_of(step):
        far = groups // 2 - (step + 1) // 2
        return lax.rem(my_group + (far if step % 2 == 0 else groups - far), groups)

    barrier = pltpu.get_barrier_semaphore()
    loads = (
        pltpu.make_async_copy(weight_in, weight_ref, load_sem.at[0]),
        pltpu.make_async_copy(dout_in, dout_ref, load_sem.at[1]),
    )
    for load in loads:
        load.start()

    @pl.loop(1, owners)
    def _(i):
        greet(barrier, plane_peer(lax.rem(me + i, owners), nd))

    @pl.loop(nd, nr)
    def _(i):
        greet(barrier, rep_peer(lax.rem(grp * nd + i, nr)))

    lane = lax.broadcasted_iota(jnp.int32, (LANES, LANES), 1)
    slot_in = ((lane % msg) // Q).astype(F32)
    piece_of = (lane[0:1, :] % Q).astype(F32)
    places = []
    for f in range(seqs):
        owner_row, rank_row, base_row = slots(owner_ref, cap, f)
        places.append(base_row)
        want = row_ref[f : f + 1, :].astype(F32) + 1.0
        row_col = column(jnp.concatenate([want, jnp.zeros_like(want)], axis=1))
        wanted = jnp.where(column(rank_row) == slot_in, row_col, 0.0).astype(BF16)
        names = onehot(iota((owners, LANES), 0) == owner_row)
        asked = jnp.dot(names, wanted, preferred_element_type=F32)
        asked = jnp.where(asked > 0.5, asked - 1.0 + piece_of * items, -1.0).astype(jnp.int32)
        for o in range(owners):
            req[o, f : f + 1, :] = asked[o : o + 1, :]

    pl.semaphore_wait(barrier, owners - 1 + nr - nd)

    @pl.loop(1, owners)
    def _(i):
        peer = lax.rem(me + i, owners)
        remote(req.at[peer], reqr.at[me], id_send, id_recv, plane_peer(peer, nd)).start()

    reqr[me] = req[me]
    hidden = hidden_ref[...].astype(F32)
    ifactor = lax.rsqrt(jnp.mean(hidden * hidden, axis=-1, keepdims=True) + EPS)
    for q in range(Q):
        cols = slice(q * piece, (q + 1) * piece)
        table[q * items : (q + 1) * items, :] = (
            hidden_ref[:, cols].astype(F32) * ifactor * igain_ref[:, cols]
        ).astype(BF16)
    remote(
        req.at[pl.ds(0, owners - 1)], reqr.at[pl.ds(0, owners - 1)], id_send, id_recv, plane_peer(me, nd)
    ).wait()

    def send_group(src, dst, f, g, send, recv):
        for k in range(per_g):
            peer = g * per_g + k

            @pl.when(peer != me)
            def _():
                remote(src.at[f, peer], dst.at[f, me], send.at[f], recv.at[f], plane_peer(peer, nd)).start()

    def all_groups(src, dst, f, send, recv):
        some = pl.ds(0, owners - 1)
        return remote(src.at[f, some], dst.at[f, some], send.at[f], recv.at[f], plane_peer(me, nd))

    lane_group = lax.broadcasted_iota(jnp.int32, (1, LANES), 1) // msg

    def fetch(f, step):
        g = turn_of(step)
        ids = jnp.zeros((1, LANES), jnp.int32)
        for k in range(per_g):
            ids = jnp.where(lane_group == k, reqr[g * per_g + k][f : f + 1, :], ids)
        val[f, g] = ids
        col = column(ids.astype(F32))
        pick = jnp.concatenate([onehot(col == iota((LANES, LANES), 1) + q * items) for q in range(Q)], axis=1)
        picked = jnp.dot(pick, table[...], preferred_element_type=F32).astype(BF16)
        out[f, pl.ds(g * per_g, per_g)] = picked.reshape(per_g, msg, piece)
        send_group(out, arr, f, g, row_send, row_recv)

    def place(f):
        arr[f, me] = out[f, me]
        base_col = column(places[f])[0:local_len]
        all_groups(out, arr, f, row_send, row_recv).wait_recv()
        arrived = arr[f].reshape(owners * msg, piece)
        total = jnp.zeros((local_len, 1), F32)
        wanted_at = jnp.concatenate([base_col + q for q in range(Q)], axis=0)
        put = jnp.concatenate(
            [onehot(iota(wanted_at.shape, 1) + t * LANES == wanted_at) for t in range(groups)], axis=1
        )
        placed = jnp.dot(put, arrived, preferred_element_type=F32)
        for q in range(Q):
            rows = placed[q * local_len : (q + 1) * local_len]
            inputs[f, :, q * piece : (q + 1) * piece] = rows.astype(BF16)
            total += jnp.sum(rows * rows, axis=-1, keepdims=True)
        factor = lax.rsqrt(total / width + EPS)
        ufactor[f] = factor
        gat[f, seq] = (inputs[f].astype(F32) * factor * ugain_ref[...]).astype(BF16)

    def give_back(f, step):
        if step == 0:
            for q in range(Q):
                stack[f, q * local_len : (q + 1) * local_len, :] = dinputs[f, :, q * piece : (q + 1) * piece]
        g = turn_of(step)
        rows = iota((LANES, LANES), 0) + (g * LANES).astype(F32)
        second = jnp.where(iota((1, LANES), 1) >= local_len, 1.0, 0.0)
        put = jnp.concatenate([onehot(rows == places[f] + (2.0 * t + second)) for t in range(Q // 2)], axis=1)
        sent = jnp.dot(put, stack[f], preferred_element_type=F32).astype(BF16)
        back_out[f, pl.ds(g * per_g, per_g)] = sent.reshape(per_g, msg, piece)
        send_group(back_out, back_arr, f, g, bk_send, bk_recv)

    def taken(f):
        back_arr[f, me] = back_out[f, me]
        for g in range(groups):
            picks[:, g * LANES : (g + 1) * LANES] = onehot(iota((Q * items, LANES), 0) == val[f, g].astype(F32))
        all_groups(back_out, back_arr, f, bk_send, bk_recv).wait_recv()
        return jnp.dot(picks[...], back_arr[f].reshape(owners * msg, piece), preferred_element_type=F32)

    def ag_place(f, d, e, origin):
        far = e // 2
        h = d if e == hops - 1 else e % 2
        block = lax.rem(origin + (ns - 2 * far if d == 0 else 2 * far), ns)
        return gat.at[f, block, pl.ds(h * hl, hl)]

    def ag_copy(f, d, e):
        ref = ag_place(f, d, e, seq)
        return remote(ref, ref, ag_send.at[f, d, e], ag_recv.at[f, d, e], ahead[d])

    def ag_arrival(f, d, e, at):
        behind = lax.rem(at + (ns - 2 if d == 0 else 2), ns)
        return ag_place(f, d, e, behind)

    def ag_wait(f, d, e):
        ref = ag_arrival(f, d, e, seq)
        remote(ref, ref, ag_send.at[f, d, e], ag_recv.at[f, d, e], ahead[d]).wait_recv()

    def sb_copy(f, n):
        ref = gat.at[f, seq] if n == 0 else ag_arrival(f, (n - 1) % 2, (n - 1) // 2, seq)
        return remote(ref, ref, sb_send.at[f, n], sb_recv.at[f, n], sib)

    def sb_wait(f, n):
        ref = gat.at[f, sib_index] if n == 0 else ag_arrival(f, (n - 1) % 2, (n - 1) // 2, sib_index)
        remote(ref, ref, sb_send.at[f, n], sb_recv.at[f, n], sib).wait_recv()

    def ag_begin(f):
        for e in range(min(2, hops)):
            for d in range(2):
                ag_copy(f, d, e).start()
        sb_copy(f, 0).start()

    def ag_event(f, d, e):
        ag_wait(f, d, e)
        if e + 2 < hops - 1:
            ag_copy(f, d, e + 2).start()
        elif e + 2 == hops - 1 + d:
            ag_copy(f, d, hops - 1).start()
        sb_copy(f, 1 + 2 * e + d).start()

    def ag_events(f):
        return [functools.partial(ag_event, f, d, e) for e in range(hops) for d in range(2)]

    def ag_end(f):
        for n in range(1 + 2 * hops):
            sb_wait(f, n)

    order = [(half, None)] + [(t, h) for t in range(half - 1, 0, -1) for h in range(2)]

    def rs_what(d, i):
        t, h = order[i]
        return t, d if h is None else h

    def chip(d, t):
        return lax.rem(z + (t if d == 0 else nz - t), nz)

    def rs_copy(f, d, i):
        t, h = rs_what(d, i)
        return remote(
            mix.at[f, chip(d, t), pl.ds(h * hl, hl)], ring.at[f, d, i], rs_send.at[f, d, i], rs_recv.at[f, d, i], ahead[d]
        )

    def mx_copy(f, k):
        return remote(part.at[f, 2 * k + 1 - core], mix.at[f, k], mx_send.at[f, k], mx_recv.at[f, k], sib)

    def own_sum(f, k):
        mix[f, k] = (mix[f, k].astype(F32) + part[f, 2 * k + core].astype(F32)).astype(BF16)

    def rs_source(d, i):
        t, h = rs_what(d, i)
        for j in range(len(order)):
            if rs_what(d, j) == (t + 1, h):
                return j
        return None

    def rs_own(f, t):
        own_sum(f, chip(0, t))
        if 0 < t < half:
            own_sum(f, chip(1, t))
        for d in range(2):
            for i in range(len(order)):
                if rs_what(d, i)[0] == t and rs_source(d, i) is None:
                    rs_copy(f, d, i).start()

    def rs_start(f):
        for k in range(nz):
            mx_copy(f, k).wait_recv()
        rs_own(f, half)
        rs_own(f, half - 1)

    def rs_event(f, d, j):
        rs_copy(f, d, j).wait_recv()
        t, h = rs_what(d, j)
        if t == 1:
            return
        for i in range(len(order)):
            if rs_what(d, i) == (t - 1, h):
                rows = pl.ds(h * hl, hl)
                k = chip(d, t - 1)
                mix[f, k, rows] = (mix[f, k, rows].astype(F32) + ring[f, d, j].astype(F32)).astype(BF16)
                rs_copy(f, d, i).start()

    def rs_events(f):
        events = [functools.partial(rs_own, f, t) for t in range(half - 2, -1, -1)]
        return events + [functools.partial(rs_event, f, d, j) for j in range(len(order)) for d in range(2)]

    def rs_end(f):
        total = mix[f, z].astype(F32)
        for h in range(2):
            rows = slice(h * hl, (h + 1) * hl)
            got = total[rows]
            for d in range(2):
                for i in range(len(order)):
                    if rs_what(d, i) == (1, h):
                        got = got + ring[f, d, i].astype(F32)
            values = inputs[f, rows, :].astype(F32)
            factor = ufactor[f, rows, :]
            weighted = ugain_ref[...] * got
            center = jnp.mean(weighted * values, axis=-1, keepdims=True)
            d_in = factor * weighted - values * (factor * factor * factor * center)
            dinputs[f, rows, :] = d_in.astype(BF16)
            for ref, term in ((uterms, got * values * factor), (iterms, d_in * values)):
                term = jnp.sum(term, axis=0, keepdims=True)
                if f == 0 and h == 0:
                    ref[...] = term
                else:
                    ref[...] += term

    def project(f, i):
        rows = gat[f, i * per : (i + 1) * per].reshape(tile, width)
        prj[f, i * tile : (i + 1) * tile, :] = jnp.dot(rows, wgt[...], preferred_element_type=F32).astype(BF16)

    def attend(f, i):
        keys_n = (i + 1) * tile
        at = slice(i * tile, (i + 1) * tile)
        query = prj[f, at, 0:HD]
        keys = prj[f, 0:keys_n, HD : 2 * HD]
        values = prj[f, 0:keys_n, 2 * HD : 3 * HD]
        upstream = dout_ref[f, at, :]
        over = (((1,), (1,)), ((), ()))
        down = (((0,), (0,)), ((), ()))
        scores = lax.dot_general(query, keys, over, preferred_element_type=F32) * scale
        p = lax.broadcasted_iota(jnp.int32, (tile, keys_n), 0) + i * tile
        k = lax.broadcasted_iota(jnp.int32, (tile, keys_n), 1)
        allowed = (k <= p) & (k < count_ref[f])
        scores = jnp.where(allowed, scores, -1e30)
        exponent = jnp.exp(scores - jnp.max(scores, axis=-1, keepdims=True))
        weights = exponent * (1.0 / jnp.sum(exponent, axis=-1, keepdims=True))
        weights_b = weights.astype(BF16)
        attn_ref[f, at, :] = jnp.dot(weights_b, values, preferred_element_type=F32).astype(BF16)
        d_weights = lax.dot_general(upstream, values, over, preferred_element_type=F32)
        center = jnp.sum(weights * d_weights, axis=-1, keepdims=True)
        d_scores = (weights * (d_weights - center) * scale).astype(BF16)
        dpr[f, at, 0:HD] = jnp.dot(d_scores, keys, preferred_element_type=F32).astype(BF16)
        d_values = lax.dot_general(weights_b, upstream, down, preferred_element_type=F32)
        d_keys = lax.dot_general(d_scores, query, down, preferred_element_type=F32)
        old = i * tile
        if i:
            dv_acc[0:old, :] += d_values[0:old]
            dk_acc[0:old, :] += d_keys[0:old]
        dv_acc[at, :] = d_values[old:]
        dk_acc[at, :] = d_keys[old:]

    def attended(f):
        dpr[f, :, HD : 2 * HD] = dk_acc[...].astype(BF16)
        dpr[f, :, 2 * HD : 3 * HD] = dv_acc[...].astype(BF16)

    def back(f, i):
        rows = dpr[f, i * tile : (i + 1) * tile, :]
        term = lax.dot_general(rows, wgt[...], (((1,), (1,)), ((), ())), preferred_element_type=F32)
        part[f, i * per : (i + 1) * per] = term.astype(BF16).reshape(per, local_len, width)
        for k in range(per // 2):
            mx_copy(f, i * per // 2 + k).start()

    def turned(f):
        dpt[:, f * length : (f + 1) * length] = dpr[f].T

    def grad(j):
        cols = slice(j * 2 * LANES, (j + 1) * 2 * LANES)
        got = jnp.zeros((dpt.shape[0], 2 * LANES), F32)
        for f in range(seqs):
            rows = gat[f, :, :, cols].reshape(length, 2 * LANES)
            got += jnp.dot(dpt[:, f * length : (f + 1) * length], rows, preferred_element_type=F32)
        for k in range(2):
            grad_out[2 * j + k] = got[:, k * LANES : (k + 1) * LANES].astype(BF16)

    gchunk = width // LANES // nr
    gmine = pl.ds(rep * gchunk, gchunk)
    gsome = pl.ds(0, (nr - 1) * gchunk)

    away = sorted(
        ((a, b) for a in range(ng) for b in range(nd) if a or b),
        key=lambda o: (min(o[0], ng - o[0]) + min(o[1], nd - o[1]), (o[0] + 2 * o[1]) % 3, o),
    )

    def rep_at(a, b):
        return lax.rem(grp + a, ng) * nd + lax.rem(dp + b, nd)

    def grads_start():
        for a, b in away:
            peer = rep_at(a, b)
            remote(grad_out.at[pl.ds(peer * gchunk, gchunk)], gin.at[rep], gr_send, gr_recv, rep_peer(peer)).start()

        gin[rep] = grad_out[gmine]

    def grads_sum():
        remote(grad_out.at[gsome], grad_out.at[gsome], gr_send, gr_recv, rep_peer(rep)).wait_recv()
        got = gin[0].astype(F32)
        for i in range(1, nr):
            got += gin[i].astype(F32)
        full_ref[gmine] = got.astype(BF16)

        for a in range(1, ng):
            gg_own(0, {"grp": lax.rem(grp + a, ng)}).start()
        for b in range(1, nd):
            gg_own(1, {"dp": lax.rem(dp + b, nd)}).start()

    def gg_own(way, device):
        return remote(full_ref.at[gmine], full_ref.at[gmine], gg_send.at[way], gg_recv.at[way], device)

    def gg_first(way):
        some = full_ref.at[pl.ds(0, (ng if way == 0 else nd) * gchunk - gchunk)]
        return remote(some, some, gg_send.at[way], gg_recv.at[way], rep_peer(rep))

    def gg_half(way):
        size = full_ref.shape[1] // 2
        return pl.ds(way * size, size)

    def gg_rest(way):
        some = full_ref.at[pl.ds(0, (ng - 1) * (nd - 1) * gchunk), gg_half(way)]
        return remote(some, some, gg_send.at[2 + way], gg_recv.at[2 + way], rep_peer(rep))

    def grads_spread():
        if ng > 1:
            gg_first(0).wait_recv()
        for a in range(1, ng):
            there = full_ref.at[pl.ds(rep_at(a, 0) * gchunk, gchunk), gg_half(0)]
            for b in range(1, nd):
                remote(there, there, gg_send.at[2], gg_recv.at[2], {"dp": lax.rem(dp + b, nd)}).start()
        if nd > 1:
            gg_first(1).wait_recv()
        for b in range(1, nd):
            there = full_ref.at[pl.ds(rep_at(0, b) * gchunk, gchunk), gg_half(1)]
            for a in range(1, ng):
                remote(there, there, gg_send.at[3], gg_recv.at[3], {"grp": lax.rem(grp + a, ng)}).start()

    def grads_end():
        for way in range(2):
            if (ng, nd)[way] > 1:
                gg_first(way).wait_send()
            if ng > 1 and nd > 1:
                gg_rest(way).wait()

    rp = 2 * Q // ns
    tsome = pl.ds(0, ns - 1)

    def gain_start():
        for q in range(Q):
            cols = slice(q * piece, (q + 1) * piece)
            tmine[q] = iterms[:, cols] / igain_ref[:, cols]
            tmine[Q + q] = uterms[:, cols]

        @pl.loop(1, ns)
        def _(i):
            peer = lax.rem(seq + i, ns)
            remote(tmine.at[pl.ds(peer * rp, rp)], tin.at[seq], t_send, t_recv, {"seq": peer}).start()

        tin[seq] = tmine[pl.ds(seq * rp, rp)]

    def gain_turn():
        remote(tin.at[tsome], tin.at[tsome], t_send, t_recv, {"seq": seq}).wait()
        total = tin[0]
        for i in range(1, ns):
            total = total + tin[i]
        tmid[rep] = total
        for a, b in away:
            remote(tmid.at[rep], tmid.at[rep], u_send, u_recv, rep_peer(rep_at(a, b))).start()

    def gain_spread():
        some = pl.ds(0, nr - 1)
        remote(tmid.at[some], tmid.at[some], u_send, u_recv, rep_peer(rep)).wait()
        total = tmid[0]
        for i in range(1, nr):
            total = total + tmid[i]
        mine = pl.ds(seq * rp, rp)
        tall[mine] = total

        @pl.loop(1, ns)
        def _(i):
            remote(tall.at[mine], tall.at[mine], v_send, v_recv, {"seq": lax.rem(seq + i, ns)}).start()

    def gain_end():
        some = pl.ds(0, (ns - 1) * rp)
        remote(tall.at[some], tall.at[some], v_send, v_recv, {"seq": seq}).wait()
        for q in range(Q):
            cols = slice(q * piece, (q + 1) * piece)
            igrad_ref[:, cols] = tall[q]
            ugrad_ref[:, cols] = tall[Q + q]

    def sequence_work(f):
        work = [functools.partial(project, f, i) for i in range(tiles)]
        work += [functools.partial(attend, f, i) for i in range(tiles)]
        work += [functools.partial(attended, f)]
        return work + [functools.partial(back, f, i) for i in range(tiles)]

    def interleave(events, work):
        done = 0
        for n, event in enumerate(events):
            event()
            upto = (n + 1) * len(work) // len(events)
            for item in work[done:upto]:
                item()
            done = upto
        for item in work[done:]:
            item()

    for f in range(seqs):
        for step in range(groups):
            fetch(f, step)
    for load in loads:
        load.wait()
    for c in range(3):
        wgt[:, c * HD : (c + 1) * HD] = weight_ref[c]
    place(0)
    ag_begin(0)
    events = ag_events(0)
    first, last = 2 * hops // 4, 2 * hops // 2
    interleave(events[:first], [])
    place(1)
    interleave(events[first:last], [])
    ag_begin(1)
    interleave(events[last:], [])
    ag_end(0)
    events = ag_events(1)
    interleave(events[:-4], sequence_work(0))
    rs_start(0)
    interleave(events[-4:], [])
    ag_end(1)
    events = rs_events(0)
    interleave(events[:-4], [functools.partial(turned, 0)] + sequence_work(1))
    rs_start(1)
    work = [functools.partial(turned, 1)] + [functools.partial(grad, j) for j in range(width // (2 * LANES))]
    interleave(events[-4:], work)
    grads_start()
    rs_end(0)
    events = rs_events(1)
    interleave(events[: len(events) // 2], [functools.partial(give_back, 0, step) for step in range(groups)])
    interleave(events[len(events) // 2 : -5], [])
    grads_sum()
    interleave(events[-5:], [])
    rs_end(1)
    gain_start()
    for step in range(groups):
        give_back(1, step)
    grads_spread()
    gain_turn()
    took = taken(0)
    gain_spread()
    took = took + taken(1)
    center = jnp.zeros((items, 1), F32)
    for q in range(Q):
        cols = slice(q * piece, (q + 1) * piece)
        h = hidden_ref[:, cols].astype(F32)
        center += jnp.sum(igain_ref[:, cols] * took[q * items : (q + 1) * items] * h, axis=-1, keepdims=True)
    center = center / width
    for q in range(Q):
        cols = slice(q * piece, (q + 1) * piece)
        h = hidden_ref[:, cols].astype(F32)
        d = took[q * items : (q + 1) * items]
        dhidden_ref[:, cols] = (
            ifactor * igain_ref[:, cols] * d - h * (ifactor * ifactor * ifactor * center)
        ).astype(BF16)
    for f in range(seqs):
        all_groups(out, arr, f, row_send, row_recv).wait_send()
        all_groups(back_out, back_arr, f, bk_send, bk_recv).wait_send()
        for d in range(2):
            for e in range(hops):
                ag_copy(f, d, e).wait_send()
                rs_copy(f, d, e).wait_send()
        for n in range(1 + 2 * hops):
            sb_copy(f, n).wait_send()
        for k in range(nz):
            mx_copy(f, k).wait_send()
    remote(grad_out.at[gsome], grad_out.at[gsome], gr_send, gr_recv, rep_peer(rep)).wait_send()
    grads_end()
    gain_end()


def main(ng, ns, nd, cap, count, owner, row, hidden, igain, ugain, weight, dout):
    items, width = hidden.shape
    seqs, local_len = row.shape
    length = ns * local_len
    owners, msg = ns * nd, cap * Q
    piece = width // Q
    nr, nz = ng * nd, ns // 2
    hops = nz - 1
    cols = 3 * HD
    vmem = pl.BlockSpec(memory_space=pltpu.VMEM)
    full = (width // LANES, cols, LANES)
    dma = pltpu.SemaphoreType.DMA
    return pl.pallas_call(
        functools.partial(main_kernel, ng, ns, nd, cap),
        out_shape=(
            jax.ShapeDtypeStruct((seqs, length, HD), BF16),
            jax.ShapeDtypeStruct((items, width), BF16),
            jax.ShapeDtypeStruct(full, BF16),
            jax.ShapeDtypeStruct((1, width), F32),
            jax.ShapeDtypeStruct((1, width), F32),
        ),
        in_specs=[pl.BlockSpec(memory_space=pltpu.SMEM)] + [vmem] * 5 + [pl.BlockSpec(memory_space=pl.ANY)] * 2,
        out_specs=[vmem] * 5,
        scratch_shapes=[
            pltpu.VMEM((owners, seqs, LANES), jnp.int32),
            pltpu.VMEM((owners, seqs, LANES), jnp.int32),
            pltpu.VMEM((seqs, owners * msg // LANES, 1, LANES), jnp.int32),
            pltpu.VMEM((Q * items, piece), BF16),
            pltpu.VMEM((seqs, owners, msg, piece), BF16),
            pltpu.VMEM((seqs, owners, msg, piece), BF16),
            pltpu.VMEM((seqs, Q * local_len, piece), BF16),
            pltpu.VMEM((seqs, owners, msg, piece), BF16),
            pltpu.VMEM((seqs, owners, msg, piece), BF16),
            pltpu.VMEM((seqs, local_len, width), BF16),
            pltpu.VMEM((seqs, local_len, 1), F32),
            pltpu.VMEM((seqs, local_len, width), BF16),
            pltpu.VMEM((1, width), F32),
            pltpu.VMEM((seqs, ns, local_len, width), BF16),
            pltpu.VMEM((seqs, length, cols), BF16),
            pltpu.VMEM((seqs, length, cols), BF16),
            pltpu.VMEM((cols, seqs * length), BF16),
            pltpu.VMEM((width, cols), BF16),
            pltpu.VMEM((seqs, ns, local_len, width), BF16),
            pltpu.VMEM((seqs, nz, local_len, width), BF16),
            pltpu.VMEM((seqs, 2, hops, local_len // 2, width), BF16),
            pltpu.VMEM((length, HD), F32),
            pltpu.VMEM((length, HD), F32),
            pltpu.VMEM(full, BF16),
            pltpu.VMEM((nr, full[0] // nr, cols, LANES), BF16),
            pltpu.VMEM((2 * Q, 1, piece), F32),
            pltpu.VMEM((ns, 2 * Q // ns, 1, piece), F32),
            pltpu.VMEM((nr, 2 * Q // ns, 1, piece), F32),
            pltpu.VMEM((2 * Q, 1, piece), F32),
            pltpu.VMEM((Q * items, owners * msg), BF16),
            pltpu.VMEM((1, width), F32),
            pltpu.VMEM(weight.shape, BF16),
            pltpu.VMEM(dout.shape, BF16),
            dma((2,)),
        ]
        + [dma] * 2
        + [dma((seqs,))] * 4
        + [dma((seqs, 2, hops))] * 2
        + [dma((seqs, 1 + 2 * hops))] * 2
        + [dma((seqs, nz))] * 2
        + [dma((seqs, 2, hops))] * 2
        + [dma] * 2
        + [dma((4,))] * 2
        + [dma] * 6,
        compiler_params=pltpu.CompilerParams(
            collective_id=0, has_side_effects=True, vmem_limit_bytes=VMEM_LIMIT
        ),
        name="main",
    )(count, owner, row, hidden, igain, ugain, weight, dout)


def finish_kernel(attn_in, dhidden_in, full_ref, ugrad_in, igrad_in, attn_ref, dhidden_ref, grad_ref, ugrad_ref, igrad_ref):
    @pl.when(pl.program_id(0) == 0)
    def _():
        attn_ref[...] = attn_in[...]
        dhidden_ref[...] = dhidden_in[...]
        ugrad_ref[...] = ugrad_in[...]
        igrad_ref[...] = igrad_in[...]

    for i in range(full_ref.shape[0]):
        grad_ref[0, i * LANES : (i + 1) * LANES, :] = full_ref[i].astype(F32).T


def finish(attn, dhidden, full, ugrad, igrad):
    chunks = full.shape[0]
    width = chunks * LANES

    def whole(a):
        return pl.BlockSpec(a.shape, lambda c: (0,) * len(a.shape))

    return pl.pallas_call(
        finish_kernel,
        grid=(3,),
        out_shape=(
            jax.ShapeDtypeStruct(attn.shape, BF16),
            jax.ShapeDtypeStruct(dhidden.shape, BF16),
            jax.ShapeDtypeStruct((3, width, HD), F32),
            jax.ShapeDtypeStruct(ugrad.shape, F32),
            jax.ShapeDtypeStruct(igrad.shape, F32),
        ),
        in_specs=[whole(attn), whole(dhidden), pl.BlockSpec((chunks, HD, LANES), lambda c: (0, c, 0)), whole(ugrad), whole(igrad)],
        out_specs=[whole(attn), whole(dhidden), pl.BlockSpec((1, width, HD), lambda c: (c, 0, 0)), whole(ugrad), whole(igrad)],
        name="finish",
    )(attn, dhidden, full, ugrad, igrad)


def local(
    item_hidden, item_gain, slot_owner, slot_row, seq_count, user_gain, query_key_value_weight, d_out
):
    ng, ns, nd = (lax.axis_size(a) for a in ("grp", "seq", "dp"))
    seqs, local_len, _ = slot_owner.shape
    width = item_hidden.shape[1]
    cap = max(2, 2 * local_len // (ns * nd))
    igain, ugain = item_gain.reshape(1, width), user_gain.reshape(1, width)
    owner = slot_owner.transpose(0, 2, 1)
    attn, d_hidden, full, ugrad, igrad = main(
        ng, ns, nd, cap, seq_count, owner, slot_row, item_hidden, igain, ugain, query_key_value_weight, d_out
    )
    attn, d_hidden, grads, ugrad, igrad = finish(attn, d_hidden, full, ugrad, igrad)
    return (attn, d_hidden, grads, ugrad.reshape(width), igrad.reshape(width))


def solution(mesh):
    in_specs = (
        P(("grp", "seq", "dp"), None),
        P(),
        P(("grp", "dp"), "seq", None),
        P(("grp", "dp"), "seq"),
        P(("grp", "dp")),
        P(),
        P(None, None, "seq"),
        P(("grp", "dp"), None, "seq"),
    )
    out_specs = (
        P(("grp", "dp"), None, "seq"),
        P(("grp", "seq", "dp"), None),
        P(None, None, "seq"),
        P(),
        P(),
    )
    return jax.shard_map(local, mesh=mesh, in_specs=in_specs, out_specs=out_specs, check_vma=False)
```
